32 devices in a mesh: row: 4 (over x, core), col: 8 (over z, y).
Axes of the slice: x: 2, y: 2, z: 4, core: 2. Of those that a mesh axis runs over, the one named last changes fastest.
Arguments:
- amps: bfloat16 [4, 8, 16, 32768], P('row', 'col'), may hold values from -6 to 6
- source: bfloat16 [4, 8, 16, 32768], P('row', 'col'), may hold values from -6 to 6
- factors: bfloat16 [16, 1024, 1024], P(None, ('row', 'col')), may hold values from -0.09375 to 0.09375
- screen: int32 [16, 8, 8], replicated, may hold values from 0 to 1, as said below
- occ_energy: float32 [4], replicated, may hold values from -1.5 to -0.3
- vir_energy: float32 [1024], replicated, may hold values from 0.2 to 2.5
Outputs:
- new_amps: bfloat16 [4, 8, 16, 32768], P('row', 'col')
The draws below stay inside these ranges and needn't reach their ends.
Inputs may be any that keep to these rules, and one draw needn't show every extreme that they name: screen[i * 4 + j, A, B] equals screen[j * 4 + i, B, A].
All inputs are finite; a program needn't handle non-finite values.
Results may differ from the reference program's by a relative error of at most 0.012.
Values may be sent and summed in bfloat16 or wider, within the bound.
A program may use at most 704 MiB of HBM per device.

```python
import jax
import jax.numpy as jnp
from jax import lax

NO = 4
PAIRS = 16
VBLK = 128
NVB = 8
NV = 1024
NQ = 16
VG = 32
ALOC = 256
TILE = 32768
N_ROW = 4
N_COL = 8


def draw_screen(key, part):
    key = jax.random.fold_in(key, 11)
    raw_levels = jax.random.randint(key, (NO, NO, NVB, NVB), 0, 3)
    summed = raw_levels + jnp.transpose(raw_levels, (1, 0, 3, 2))
    return (summed >= 2).astype(jnp.int32).reshape(NO * NO, NVB, NVB)


def levels(stream_key, shape, cuts, smallest, top_value):
    factor_of = 1.0
    for position, shards_of in cuts:
        steps = jax.random.uniform(jax.random.fold_in(jax.random.fold_in(stream_key, 6), position), (shards_of,), jnp.float32, smallest / len(cuts), top_value / len(cuts))
        factor_of = factor_of * jnp.repeat(jnp.exp(steps), shape[position] // shards_of).reshape((-1,) + (1,) * (len(shape) - 1 - position))
    return factor_of


def scatter_about(key, extent, deviation, limit, split=(), dtype=jnp.bfloat16):
    result = deviation * jax.random.normal(key, extent, jnp.float32)
    if split:
        result = result * levels(key, extent, split, -0.22, 0.18)
    return jnp.clip(result, -limit, limit).astype(dtype)


def setup_inputs(seed: int = 0) -> dict:
    streams_of = jax.random.split(jax.random.key(seed), 7)
    amps = scatter_about(streams_of[0], (N_ROW, N_COL, PAIRS, TILE), 1.0, 6.0, ((0, 4), (1, 8)))
    source = scatter_about(streams_of[1], (N_ROW, N_COL, PAIRS, TILE), 1.0, 6.0, ((0, 4), (1, 8)))
    factors = scatter_about(streams_of[2], (NQ, NV, NV), (4 * NV) ** -0.5, 0.09375, ((1, 32),))
    screen = draw_screen(jax.random.fold_in(streams_of[6], 71), 0)
    occ_energy = jnp.clip(jax.random.uniform(streams_of[4], (NO,), jnp.float32, -1.5, -0.3), -1.5, -0.3)
    vir_energy = jnp.clip(jax.random.uniform(streams_of[5], (NV,), jnp.float32, 0.2, 2.5), 0.2, 2.5)
    return dict(amps=amps, source=source, factors=factors, screen=screen, occ_energy=occ_energy, vir_energy=vir_energy)


def to_dense(blocked):
    shaped = blocked.reshape(N_ROW, N_COL, PAIRS, ALOC, N_ROW, VG)
    return shaped.transpose(2, 0, 3, 4, 1, 5).reshape(PAIRS, NV, NV)


def to_blocked(dense):
    shaped = dense.reshape(PAIRS, N_ROW, ALOC, N_ROW, N_COL, VG)
    return shaped.transpose(1, 4, 0, 2, 3, 5).reshape(N_ROW, N_COL, PAIRS, TILE)


def reference(amps, source, factors, screen, occ_energy, vir_energy):
    dense_amps = to_dense(amps.astype(jnp.float32))
    dense_source = to_dense(source.astype(jnp.float32))
    block_of = jnp.arange(NV) // VBLK
    mask_full = screen.astype(jnp.float32)[:, block_of][:, :, block_of]
    screened = (dense_amps * mask_full).astype(jnp.bfloat16).astype(jnp.float32)
    factor_full = factors.astype(jnp.float32)

    def accumulate(aux_id, running):
        factor = factor_full[aux_id]
        inner_part = jnp.einsum('pcd,bd->pcb', screened, factor).astype(jnp.bfloat16)
        inner_part = lax.optimization_barrier(inner_part).astype(jnp.float32)
        return running + jnp.einsum('ac,pcb->pab', factor, inner_part)

    ladder = lax.fori_loop(0, NQ, accumulate, jnp.zeros((PAIRS, NV, NV), jnp.float32))
    resid = dense_source + ladder
    swapped = resid.reshape(NO, NO, NV, NV).transpose(1, 0, 3, 2).reshape(PAIRS, NV, NV)
    rsym = resid + swapped
    occ_pair = (occ_energy[:, None] + occ_energy[None, :]).reshape(PAIRS)
    denom = occ_pair[:, None, None] - vir_energy[None, :, None] - vir_energy[None, None, :]
    updated = mask_full * (dense_amps + rsym / denom)
    return to_blocked(updated.astype(jnp.bfloat16))
```

```python
import functools

import jax
import jax.numpy as jnp
from jax import lax
from jax.experimental import pallas as pl
from jax.experimental.pallas import tpu as pltpu
from jax.sharding import PartitionSpec as P

VMEM = pltpu.VMEM
LANES = 128


def pair_table(occ_count):
    table = []
    for i in range(occ_count):
        for j in range(i + 1, occ_count):
            table.append((i * occ_count + j, j * occ_count + i))
    for i in range(0, occ_count, 2):
        table.append((i * occ_count + i, (i + 1) * occ_count + i + 1))
    return table


def whole(count):
    return [pl.BlockSpec(memory_space=VMEM)] * count


def pack_kernel(table, amps_ref, source_ref, mask_ref, tm_ref, s_ref, rows):
    pair_count, a_local = rows.shape[0], rows.shape[1]
    groups, group = tm_ref.shape[2], tm_ref.shape[3]
    half_len = a_local // mask_ref.shape[0]

    def turn(in_ref, out_ref, masked):
        for half in range(mask_ref.shape[0]):

            @pl.loop(0, half_len, unroll=8)
            def _(step):
                x = half * half_len + step
                one = in_ref[:, pl.ds(pl.multiple_of(x * LANES, LANES), LANES)].astype(jnp.float32)
                if masked:
                    one = one * mask_ref[half]
                rows[:, x, :] = one

        for dest, pairs in enumerate(table):
            for slot, pair in enumerate(pairs):
                turned = rows[pair].T.astype(jnp.bfloat16)
                out_ref[dest, slot] = turned.reshape(groups, group, a_local)

    turn(amps_ref, tm_ref, True)
    turn(source_ref, s_ref, False)


def ladder_kernel(last, *refs):
    if last:
        t_ref, b_ref, prior_ref, out_ref, total, t_all, b_all, inner, t_sem, b_sem, p_sem = refs
    else:
        t_ref, b_ref, out_ref, t_all, b_all, inner, t_sem, b_sem = refs
        total = out_ref
    row_count, col_count, slots = t_ref.shape[0], t_ref.shape[1], t_ref.shape[2]
    a_local = t_ref.shape[5]
    q_count = b_ref.shape[2]
    virt = b_ref.shape[4]
    block = 512 if virt % 512 == 0 else virt
    blocks = virt // block
    rows_per = block // (virt // row_count)

    b_copies = [
        [
            pltpu.make_async_copy(b_ref.at[c, :, q], b_all.at[q, :, c], b_sem.at[q, c])
            for c in range(col_count)
        ]
        for q in range(q_count)
    ]
    t_copies = [
        pltpu.make_async_copy(
            t_ref.at[r, c, p],
            t_all.at[p, :, c, :, pl.ds(r * a_local, a_local)],
            t_sem.at[r, c, p],
        )
        for p in range(slots)
        for c in range(col_count)
        for r in range(row_count)
    ]
    for copy in b_copies[0] + t_copies:
        copy.start()
    for some in b_copies[1:]:
        for copy in some:
            copy.start()
    if last:
        prior_copy = pltpu.make_async_copy(prior_ref, total, p_sem)
        prior_copy.start()
    for copy in t_copies:
        copy.wait()

    for q in range(q_count):
        for copy in b_copies[q]:
            copy.wait()
        if q == 0 and last:
            prior_copy.wait()
        for p in range(slots):

            @pl.loop(0, blocks * blocks)
            def _(step):
                m, n = step // blocks, step % blocks
                left = b_all[q, pl.ds(m * rows_per, rows_per)].reshape(block, virt)
                cols = pl.ds(pl.multiple_of(n * block, block), block)
                right = t_all[p, :, :, :, cols].reshape(virt, block)
                inner[pl.ds(pl.multiple_of(m * block, block), block), cols] = jnp.dot(
                    left, right, preferred_element_type=jnp.float32
                ).astype(jnp.bfloat16)

            @pl.loop(0, blocks * blocks)
            def _(step):
                m, n = step // blocks, step % blocks
                some = pl.ds(pl.multiple_of(m * block, block), block)
                cols = pl.ds(pl.multiple_of(n * block, block), block)
                right = b_all[q, pl.ds(n * rows_per, rows_per)].reshape(block, virt)
                part = lax.dot_general(
                    inner[some, :],
                    right,
                    (((1,), (1,)), ((), ())),
                    preferred_element_type=jnp.float32,
                )
                if q > 0 or last:
                    part = part + total[p, some, cols]
                if last and q == q_count - 1:
                    for k in range(rows_per):
                        out_ref[n * rows_per + k, p, some, :] = part[
                            :, k * a_local : (k + 1) * a_local
                        ].astype(jnp.bfloat16)
                else:
                    total[p, some, cols] = part


def resid_kernel(ladder_ref, s_ref, resid_ref, swap_ref):
    col_count, slots, row_count, group, a_local = s_ref.shape
    for p in range(slots):
        for y in range(row_count):
            for c in range(col_count):
                some = pl.ds(y * a_local + c * group, group)
                resid_ref[p, some, :] = s_ref[c, p, y].astype(jnp.float32) + ladder_ref[
                    p, some, :
                ].astype(jnp.float32)
            swap_ref[y, p] = resid_ref[p, pl.ds(y * a_local, a_local), :].T.astype(jnp.bfloat16)


def add_kernel(diagonal_from, resid_ref, swap_ref, out_ref):
    col_count, slots, row_count, group, a_local = out_ref.shape
    flip = (lax.axis_index("col") < diagonal_from).astype(jnp.int32)
    for p in range(slots):
        partner = p * (1 - flip) + (slots - 1 - p) * flip
        for y in range(row_count):
            for c in range(col_count):
                some = pl.ds(y * a_local + c * group, group)
                other = swap_ref[y, partner, pl.ds(c * group, group), :]
                both = resid_ref[p, some, :] + other.astype(jnp.float32)
                out_ref[c, p, y] = both.astype(jnp.bfloat16)


def update_kernel(table, amps_ref, rsym_ref, mask_ref, occ_ref, vir_b_ref, vir_a_ref, out_ref, rows):
    pair_count, a_local = rows.shape[0], rows.shape[1]
    half_len = a_local // mask_ref.shape[0]
    for owner, pairs in enumerate(table):
        for slot, pair in enumerate(pairs):
            one = rsym_ref[owner, slot].reshape(LANES, a_local).astype(jnp.float32)
            rows[pair] = one.T
    known = occ_ref[...] - vir_b_ref[...]
    for half in range(mask_ref.shape[0]):

        @pl.loop(0, half_len, unroll=8)
        def _(step):
            x = half * half_len + step
            lanes = pl.ds(pl.multiple_of(x * LANES, LANES), LANES)
            denom = known - vir_a_ref[x]
            new = mask_ref[half] * (amps_ref[:, lanes].astype(jnp.float32) + rows[:, x, :] / denom)
            out_ref[:, lanes] = new.astype(jnp.bfloat16)


def params(limit=56):
    return pltpu.CompilerParams(vmem_limit_bytes=limit * 1024 * 1024)


def fast_shards(amps, source, factors, screen, occ_energy, vir_energy):
    row_count = lax.axis_size("row")
    col_count = lax.axis_size("col")
    row_id = lax.axis_index("row")
    col_id = lax.axis_index("col")
    pair_count = amps.shape[2]
    aux_count, group, virt = factors.shape
    a_local = col_count * group
    b_local = row_count * group
    occ_count = occ_energy.shape[0]
    block_count = screen.shape[1]
    block_size = virt // block_count
    halves = a_local // block_size
    per_y = block_count // row_count
    slots = pair_count // col_count
    share = aux_count // row_count
    table = pair_table(occ_count)
    bf16, f32 = jnp.bfloat16, jnp.float32

    amps = amps.reshape(pair_count, a_local * b_local)
    source = source.reshape(pair_count, a_local * b_local)
    mine = lax.dynamic_slice_in_dim(screen, row_id * halves, halves, 1)
    mine = mine.reshape(pair_count, halves, row_count, per_y)
    mine = lax.dynamic_slice_in_dim(mine, col_id * group // block_size, 1, 3)
    mask = jnp.broadcast_to(
        mine.transpose(1, 0, 2, 3).astype(f32), (halves, pair_count, row_count, group)
    ).reshape(halves, pair_count, b_local)
    occ_pair = (occ_energy[:, None] + occ_energy[None, :]).reshape(pair_count, 1)
    vir_a = lax.dynamic_slice_in_dim(vir_energy, row_id * a_local, a_local)
    vir_b = lax.dynamic_slice_in_dim(
        vir_energy.reshape(row_count, col_count, group), col_id, 1, 1
    ).reshape(1, b_local)

    chunks = 2
    per_chunk = share // chunks
    by_share = factors.reshape(row_count, chunks, per_chunk, group, virt)
    gathered = []
    for k in range(chunks):
        rows_of = lax.all_to_all(by_share[:, k], "row", split_axis=0, concat_axis=0, tiled=True)
        gathered.append(lax.all_gather(rows_of, "col", axis=0))

    block = (col_count, slots, row_count, group, a_local)
    tm_blocks, s_blocks = pl.pallas_call(
        functools.partial(pack_kernel, table),
        out_shape=[jax.ShapeDtypeStruct(block, bf16)] * 2,
        in_specs=whole(3),
        out_specs=whole(2),
        scratch_shapes=[VMEM((pair_count, a_local, LANES), f32)],
        compiler_params=params(),
        name="pack_tiles",
    )(amps, source, mask)
    tm_mine = lax.all_to_all(tm_blocks, "col", split_axis=0, concat_axis=0, tiled=True)
    s_mine = lax.all_to_all(s_blocks, "col", split_axis=0, concat_axis=0, tiled=True)
    tm_all = lax.all_gather(tm_mine, "row", axis=0)

    flops = 4 * per_chunk * slots * virt**3
    prior = None
    for k in range(chunks):
        last = k == chunks - 1
        operands = [tm_all, gathered[k]] + ([prior] if last else [])
        total = (slots, virt, virt)
        prior = pl.pallas_call(
            functools.partial(ladder_kernel, last),
            out_shape=(
                jax.ShapeDtypeStruct((row_count, slots, virt, a_local), bf16)
                if last
                else jax.ShapeDtypeStruct(total, f32)
            ),
            in_specs=[pl.BlockSpec(memory_space=pl.ANY)] * len(operands),
            out_specs=pl.BlockSpec(memory_space=VMEM),
            scratch_shapes=([VMEM(total, f32)] if last else [])
            + [
                VMEM((slots, row_count, col_count, group, virt), bf16),
                VMEM((per_chunk, row_count, col_count, group, virt), bf16),
                VMEM((virt, virt), bf16),
                pltpu.SemaphoreType.DMA((row_count, col_count, slots)),
                pltpu.SemaphoreType.DMA((per_chunk, col_count)),
            ]
            + ([pltpu.SemaphoreType.DMA] if last else []),
            compiler_params=params(),
            cost_estimate=pl.CostEstimate(
                flops=flops, bytes_accessed=16 * 1024 * 1024, transcendentals=0
            ),
            name="ladder_end" if last else "ladder_begin",
        )(*operands)

    ladder = lax.psum_scatter(prior, "row", scatter_dimension=0, tiled=True)
    ladder = ladder.reshape(slots, virt, a_local)
    resid, swap = pl.pallas_call(
        resid_kernel,
        out_shape=[
            jax.ShapeDtypeStruct((slots, virt, a_local), f32),
            jax.ShapeDtypeStruct((row_count, slots, a_local, a_local), bf16),
        ],
        in_specs=whole(2),
        out_specs=whole(2),
        compiler_params=params(),
        name="resid",
    )(ladder, s_mine)
    swapped = lax.all_to_all(swap, "row", split_axis=0, concat_axis=0, tiled=True)
    rsym = pl.pallas_call(
        functools.partial(add_kernel, occ_count * (occ_count - 1) // 2),
        out_shape=jax.ShapeDtypeStruct(block, bf16),
        in_specs=whole(2),
        out_specs=whole(1)[0],
        compiler_params=params(),
        name="add_swapped",
    )(resid, swapped)
    rsym = lax.all_to_all(rsym, "col", split_axis=0, concat_axis=0, tiled=True)
    new = pl.pallas_call(
        functools.partial(update_kernel, table),
        out_shape=jax.ShapeDtypeStruct((pair_count, a_local * b_local), bf16),
        in_specs=whole(5) + [pl.BlockSpec(memory_space=pltpu.SMEM)],
        out_specs=whole(1)[0],
        scratch_shapes=[VMEM((pair_count, a_local, LANES), f32)],
        compiler_params=params(),
        name="update",
    )(amps, rsym, mask, occ_pair, vir_b, vir_a)
    return new.reshape(1, 1, pair_count, a_local * b_local)


def to_col_major(array, dim, row_count, col_count):
    old_shape = array.shape
    group_len = old_shape[dim] // (row_count * col_count)
    divided = array.reshape(
        old_shape[:dim] + (row_count, col_count, group_len) + old_shape[dim + 1 :]
    )
    return jnp.swapaxes(divided, dim, dim + 1).reshape(old_shape)


def ladder_over_aux(running, segment, left_part, right_factor):

    def step(total, factor_pair):
        left_one, right_one = factor_pair
        inner_part = jnp.einsum(
            "pcd,bd->pcb", segment, right_one, preferred_element_type=jnp.float32
        ).astype(jnp.bfloat16)
        return (
            total
            + jnp.einsum("ac,pcb->pab", left_one, inner_part, preferred_element_type=jnp.float32),
            None,
        )

    result, unused = lax.scan(step, running, (left_part, right_factor))
    return result


def shards(amps, source, factors, screen, occ_energy, vir_energy):
    row_count = lax.axis_size("row")
    col_count = lax.axis_size("col")
    row_id = lax.axis_index("row")
    col_id = lax.axis_index("col")
    pair_count = amps.shape[2]
    aux_count, group_size, virt_count = factors.shape
    a_local = col_count * group_size
    b_local = row_count * group_size
    occ_count = occ_energy.shape[0]
    block_count = screen.shape[1]
    block_size = virt_count // block_count
    a_index = row_id * a_local + jnp.arange(a_local)
    b_position = jnp.arange(b_local)
    b_index = b_position // group_size * a_local + col_id * group_size + b_position % group_size
    block_ids = jnp.arange(block_count)
    select_rows = (a_index[:, None] // block_size == block_ids[None, :]).astype(jnp.float32)
    select_cols = (b_index[:, None] // block_size == block_ids[None, :]).astype(jnp.float32)
    mask_tile = jnp.einsum("pxy,ax,by->pab", screen.astype(jnp.float32), select_rows, select_cols)
    amp_tile = amps.reshape(pair_count, a_local, b_local)
    masked = (amp_tile * mask_tile).astype(jnp.bfloat16)
    share_rows = lax.all_to_all(factors, "row", split_axis=0, concat_axis=1, tiled=True)
    col_ordered = lax.all_gather(share_rows, "col", axis=1, tiled=True)
    left_factor = to_col_major(col_ordered, 1, col_count, row_count)
    right_factor = to_col_major(col_ordered, 2, row_count, col_count)
    mine = lax.all_to_all(masked, "col", split_axis=0, concat_axis=2, tiled=True)
    initial = jnp.zeros((mine.shape[0], virt_count, virt_count), jnp.float32)
    ladder_sum = ladder_over_aux(
        initial, lax.all_gather(mine, "row", axis=1, tiled=True), left_factor, right_factor
    )
    reduced = lax.psum_scatter(
        ladder_sum.astype(jnp.bfloat16), "row", scatter_dimension=1, tiled=True
    ).astype(jnp.float32)
    ladder = lax.all_to_all(
        reduced.astype(jnp.bfloat16), "col", split_axis=2, concat_axis=0, tiled=True
    ).astype(reduced.dtype)
    resid = source.reshape(pair_count, a_local, b_local).astype(jnp.float32) + ladder
    split_tile = resid.reshape(pair_count, col_count, group_size, row_count, group_size)
    received = lax.all_to_all(
        lax.all_to_all(
            split_tile.astype(jnp.bfloat16), "row", split_axis=3, concat_axis=3, tiled=True
        ),
        "col",
        split_axis=1,
        concat_axis=1,
        tiled=True,
    ).astype(split_tile.dtype)
    swapped = received.transpose(0, 1, 4, 3, 2).reshape(occ_count, occ_count, a_local, b_local)
    swapped = swapped.transpose(1, 0, 2, 3).reshape(pair_count, a_local, b_local)
    rsym = resid + swapped
    occ_pair = (occ_energy[:, None] + occ_energy[None, :]).reshape(pair_count)
    vir_rows = lax.dynamic_slice_in_dim(vir_energy, row_id * a_local, a_local)
    vir_cols = lax.dynamic_slice_in_dim(
        vir_energy.reshape(row_count, col_count, group_size), col_id, 1, 1
    ).reshape(b_local)
    denominator = occ_pair[:, None, None] - vir_rows[None, :, None] - vir_cols[None, None, :]
    updated = mask_tile * (amp_tile.astype(jnp.float32) + rsym / denominator)
    return updated.astype(jnp.bfloat16).reshape(1, 1, pair_count, a_local * b_local)


def fits(amps, factors, screen, occ_energy, row_count, col_count):
    aux_count, rows, virt = factors.shape
    group = rows // (row_count * col_count)
    a_local, b_local = col_count * group, row_count * group
    block_size = virt // screen.shape[1]
    occ_count = occ_energy.shape[0]
    return (
        group % 16 == 0
        and b_local == LANES
        and a_local % LANES == 0
        and block_size % group == 0
        and a_local % block_size == 0
        and occ_count % 2 == 0
        and 2 * col_count == occ_count * occ_count
        and amps.shape[2] == occ_count * occ_count
        and aux_count % (2 * row_count) == 0
        and virt % 512 == 0
        and 512 % a_local == 0
    )


def solution(mesh):
    in_specs = (
        P("row", "col", None, None),
        P("row", "col", None, None),
        P(None, ("row", "col"), None),
        P(),
        P(),
        P(),
    )
    out_specs = P("row", "col", None, None)
    row_count, col_count = mesh.shape["row"], mesh.shape["col"]

    def run(amps, source, factors, screen, occ_energy, vir_energy):
        fast = fits(amps, factors, screen, occ_energy, row_count, col_count)
        body = fast_shards if fast else shards
        return jax.shard_map(
            body, mesh=mesh, in_specs=in_specs, out_specs=out_specs, check_vma=False
        )(amps, source, factors, screen, occ_energy, vir_energy)

    return run
```

```python
import functools

import jax
import jax.numpy as jnp
from jax import lax
from jax.experimental import pallas as pl
from jax.experimental.pallas import tpu as pltpu
from jax.sharding import PartitionSpec as P

VMEM = pltpu.VMEM
LANES = 128


def pair_table(occ_count):
    table = []
    for i in range(occ_count):
        for j in range(i + 1, occ_count):
            table.append((i * occ_count + j, j * occ_count + i))
    for i in range(0, occ_count, 2):
        table.append((i * occ_count + i, (i + 1) * occ_count + i + 1))
    return table


def whole(count):
    return [pl.BlockSpec(memory_space=VMEM)] * count


def pack_kernel(table, amps_ref, source_ref, mask_ref, tm_ref, s_ref, rows):
    pair_count, a_local = rows.shape[0], rows.shape[1]
    groups, group = tm_ref.shape[2], tm_ref.shape[3]
    half_len = a_local // mask_ref.shape[0]

    def turn(in_ref, out_ref, masked):
        for half in range(mask_ref.shape[0]):

            @pl.loop(0, half_len, unroll=8)
            def _(step):
                x = half * half_len + step
                one = in_ref[:, pl.ds(pl.multiple_of(x * LANES, LANES), LANES)].astype(jnp.float32)
                if masked:
                    one = one * mask_ref[half]
                rows[:, x, :] = one

        for dest, pairs in enumerate(table):
            for slot, pair in enumerate(pairs):
                turned = rows[pair].T.astype(jnp.bfloat16)
                out_ref[dest, slot] = turned.reshape(groups, group, a_local)

    turn(amps_ref, tm_ref, True)
    turn(source_ref, s_ref, False)


def ring_column(position, count):
    position = (position + count) % count
    back = position // (count // 2)
    return (1 - back) * 2 * position + back * (2 * (count - 1 - position) + 1)


def ladder_kernel(
    tm_ref,
    factors_ref,
    out_ref,
    t_all,
    b_all,
    inner,
    total,
    near_sem,
    share_send,
    share_recv,
    tile_send,
    tile_recv,
    slab_send,
    slab_recv,
    ring_send,
    ring_recv,
):
    q_count, row_count, col_count, group, virt = b_all.shape
    slots, a_local = t_all.shape[1], t_all.shape[5]
    row, col = lax.axis_index("row"), lax.axis_index("col")
    sibling = row + 1 - 2 * (row % 2)
    across = (row + 2) % row_count
    place = (col // 2) * (1 - col % 2) + (col_count - 1 - col // 2) * (col % 2)
    half_rows = row_count // 2

    def remote(source, dest, send_sem, recv_sem, device):
        return pltpu.make_async_remote_copy(
            src_ref=source,
            dst_ref=dest,
            send_sem=send_sem,
            recv_sem=recv_sem,
            device_id=device,
            device_id_type=pl.DeviceIdType.MESH,
        )

    barrier = pltpu.get_barrier_semaphore()
    for step in range(1, row_count):
        pl.semaphore_signal(
            barrier,
            inc=1,
            device_id={"row": (row + step) % row_count},
            device_id_type=pl.DeviceIdType.MESH,
        )
    for step in range(1, col_count):
        pl.semaphore_signal(
            barrier,
            inc=1,
            device_id={"col": (col + step) % col_count},
            device_id_type=pl.DeviceIdType.MESH,
        )
    pl.semaphore_wait(barrier, row_count + col_count - 2)

    def share_copy(q, step):
        to_row = (row + step) % row_count
        return remote(
            factors_ref.at[to_row, q],
            b_all.at[q, row, col],
            share_send.at[q, step - 1],
            share_recv.at[q, step - 1],
            {"row": to_row},
        )

    def share_arrival(q, step):
        from_row = (row + row_count - step) % row_count
        here = b_all.at[q, from_row, col]
        return remote(here, here, share_send.at[q, step - 1], share_recv.at[q, step - 1], {"row": from_row})

    def tile_copy(step):
        to_col = (col + step) % col_count
        return remote(
            tm_ref.at[to_col],
            t_all.at[row, :, :, col],
            tile_send.at[step - 1],
            tile_recv.at[step - 1],
            {"col": to_col},
        )

    def tile_arrival(step):
        from_col = (col + col_count - step) % col_count
        here = t_all.at[row, :, :, from_col]
        return remote(here, here, tile_send.at[step - 1], tile_recv.at[step - 1], {"col": from_col})

    def slab_copy(kind):
        slab = t_all.at[(row, row, across)[kind]]
        to_row = (sibling, across, sibling)[kind]
        return remote(slab, slab, slab_send.at[kind], slab_recv.at[kind], {"row": to_row})

    def slab_arrival(kind):
        slab = t_all.at[(sibling, across, (sibling + 2) % row_count)[kind]]
        return remote(slab, slab, slab_send.at[kind], slab_recv.at[kind], {"row": sibling})

    def hops(q, way):
        return col_count // 2 - (q + way) % 2

    def ring_block(q, half, position):
        return b_all.at[q, pl.ds(half * half_rows, half_rows), ring_column(position, col_count)]

    def ring_copy(way, q, half, hop):
        sign = 1 - 2 * way
        block = ring_block(q, half, place - sign * hop)
        to_col = ring_column(place + sign, col_count)
        sems = ring_send.at[way, q, half, hop], ring_recv.at[way, q, half, hop]
        return remote(block, block, *sems, {"col": to_col})

    def ring_arrival(way, q, half, hop):
        sign = 1 - 2 * way
        block = ring_block(q, half, place - sign * (hop + 1))
        to_col = ring_column(place + sign, col_count)
        sems = ring_send.at[way, q, half, hop], ring_recv.at[way, q, half, hop]
        return remote(block, block, *sems, {"col": to_col})

    def ring_begin(q):
        for step in range(1, row_count):
            share_arrival(q, step).wait_recv()
        near_share[q].wait()
        for half in range(2):
            for way in range(2):
                ring_copy(way, q, half, 0).start()

    def ring_step(q, hop):
        for half in range(2):
            for way in range(2):
                if hop < hops(q, way):
                    ring_arrival(way, q, half, hop).wait_recv()
                    if hop + 1 < hops(q, way):
                        ring_copy(way, q, half, hop + 1).start()

    near_share = [
        pltpu.make_async_copy(factors_ref.at[row, q], b_all.at[q, row, col], near_sem.at[q])
        for q in range(q_count)
    ]
    near_tile = pltpu.make_async_copy(
        tm_ref.at[col], t_all.at[row, :, :, col], near_sem.at[q_count]
    )
    for q in range(q_count):
        near_share[q].start()
        for step in range(1, row_count):
            share_copy(q, step).start()
    near_tile.start()
    for step in range(1, col_count):
        tile_copy(step).start()

    block = 512
    blocks = virt // block
    rows_per = block // a_local
    ring_hops = col_count // 2

    ring_begin(0)
    ring_begin(1)
    ring_step(0, 0)
    for step in range(1, col_count):
        tile_arrival(step).wait_recv()
    near_tile.wait()
    slab_copy(0).start()
    slab_copy(1).start()
    for hop in range(1, ring_hops - 1):
        ring_step(0, hop)
    slab_arrival(1).wait_recv()
    slab_copy(2).start()
    ring_step(0, ring_hops - 1)
    slab_arrival(0).wait_recv()
    slab_arrival(2).wait_recv()

    for q in range(q_count):
        if q + 2 < q_count:
            ring_begin(q + 2)
        hop_done = 0
        for p in range(slots):

            @pl.loop(0, blocks * row_count)
            def _(step):
                m, n = step // row_count, step % row_count
                left = b_all[q, pl.ds(m * rows_per, rows_per)].reshape(block, virt)
                right = t_all[n, p].reshape(virt, a_local)
                inner[
                    pl.ds(pl.multiple_of(m * block, block), block),
                    pl.ds(pl.multiple_of(n * a_local, a_local), a_local),
                ] = jnp.dot(left, right, preferred_element_type=jnp.float32).astype(jnp.bfloat16)

            if q + 1 < q_count and hop_done < ring_hops:
                ring_step(q + 1, hop_done)
                hop_done += 1

            @pl.loop(0, blocks * blocks)
            def _(step):
                m, n = step // blocks, step % blocks
                some = pl.ds(pl.multiple_of(m * block, block), block)
                cols = pl.ds(pl.multiple_of(n * block, block), block)
                right = b_all[q, pl.ds(n * rows_per, rows_per)].reshape(block, virt)
                part = lax.dot_general(
                    inner[some, :],
                    right,
                    (((1,), (1,)), ((), ())),
                    preferred_element_type=jnp.float32,
                )
                if q > 0:
                    part = part + total[p, some, cols]
                if q == q_count - 1:
                    for k in range(rows_per):
                        out_ref[n * rows_per + k, p, some, :] = part[
                            :, k * a_local : (k + 1) * a_local
                        ].astype(jnp.bfloat16)
                else:
                    total[p, some, cols] = part

            if q + 1 < q_count and hop_done < ring_hops:
                ring_step(q + 1, hop_done)
                hop_done += 1
        if q + 1 < q_count:
            for hop in range(hop_done, ring_hops):
                ring_step(q + 1, hop)

    for q in range(q_count):
        for step in range(1, row_count):
            share_copy(q, step).wait_send()
        for half in range(2):
            for way in range(2):
                for hop in range(hops(q, way)):
                    ring_copy(way, q, half, hop).wait_send()
    for step in range(1, col_count):
        tile_copy(step).wait_send()
    for kind in range(3):
        slab_copy(kind).wait_send()


def resid_kernel(ladder_ref, s_ref, resid_ref, swap_ref):
    col_count, slots, row_count, group, a_local = s_ref.shape
    for p in range(slots):
        for y in range(row_count):
            for c in range(col_count):
                some = pl.ds(y * a_local + c * group, group)
                resid_ref[p, some, :] = s_ref[c, p, y].astype(jnp.float32) + ladder_ref[
                    p, some, :
                ].astype(jnp.float32)
            swap_ref[y, p] = resid_ref[p, pl.ds(y * a_local, a_local), :].T.astype(jnp.bfloat16)


def add_kernel(diagonal_from, resid_ref, swap_ref, out_ref):
    col_count, slots, row_count, group, a_local = out_ref.shape
    flip = (lax.axis_index("col") < diagonal_from).astype(jnp.int32)
    for p in range(slots):
        partner = p * (1 - flip) + (slots - 1 - p) * flip
        for y in range(row_count):
            for c in range(col_count):
                some = pl.ds(y * a_local + c * group, group)
                other = swap_ref[y, partner, pl.ds(c * group, group), :]
                both = resid_ref[p, some, :] + other.astype(jnp.float32)
                out_ref[c, p, y] = both.astype(jnp.bfloat16)


def update_kernel(table, amps_ref, rsym_ref, mask_ref, occ_ref, vir_b_ref, vir_a_ref, out_ref, rows):
    pair_count, a_local = rows.shape[0], rows.shape[1]
    half_len = a_local // mask_ref.shape[0]
    for owner, pairs in enumerate(table):
        for slot, pair in enumerate(pairs):
            one = rsym_ref[owner, slot].reshape(LANES, a_local).astype(jnp.float32)
            rows[pair] = one.T
    known = occ_ref[...] - vir_b_ref[...]
    for half in range(mask_ref.shape[0]):

        @pl.loop(0, half_len, unroll=8)
        def _(step):
            x = half * half_len + step
            lanes = pl.ds(pl.multiple_of(x * LANES, LANES), LANES)
            denom = known - vir_a_ref[x]
            new = mask_ref[half] * (amps_ref[:, lanes].astype(jnp.float32) + rows[:, x, :] / denom)
            out_ref[:, lanes] = new.astype(jnp.bfloat16)


def params(limit=56):
    return pltpu.CompilerParams(vmem_limit_bytes=limit * 1024 * 1024)


def fast_shards(amps, source, factors, screen, occ_energy, vir_energy):
    row_count = lax.axis_size("row")
    col_count = lax.axis_size("col")
    row_id = lax.axis_index("row")
    col_id = lax.axis_index("col")
    pair_count = amps.shape[2]
    aux_count, group, virt = factors.shape
    a_local = col_count * group
    b_local = row_count * group
    occ_count = occ_energy.shape[0]
    block_count = screen.shape[1]
    block_size = virt // block_count
    halves = a_local // block_size
    per_y = block_count // row_count
    slots = pair_count // col_count
    share = aux_count // row_count
    table = pair_table(occ_count)
    bf16, f32 = jnp.bfloat16, jnp.float32

    amps = amps.reshape(pair_count, a_local * b_local)
    source = source.reshape(pair_count, a_local * b_local)
    mine = lax.dynamic_slice_in_dim(screen, row_id * halves, halves, 1)
    mine = mine.reshape(pair_count, halves, row_count, per_y)
    mine = lax.dynamic_slice_in_dim(mine, col_id * group // block_size, 1, 3)
    mask = jnp.broadcast_to(
        mine.transpose(1, 0, 2, 3).astype(f32), (halves, pair_count, row_count, group)
    ).reshape(halves, pair_count, b_local)
    occ_pair = (occ_energy[:, None] + occ_energy[None, :]).reshape(pair_count, 1)
    vir_a = lax.dynamic_slice_in_dim(vir_energy, row_id * a_local, a_local)
    vir_b = lax.dynamic_slice_in_dim(
        vir_energy.reshape(row_count, col_count, group), col_id, 1, 1
    ).reshape(1, b_local)

    block = (col_count, slots, row_count, group, a_local)
    tm_blocks, s_blocks = pl.pallas_call(
        functools.partial(pack_kernel, table),
        out_shape=[jax.ShapeDtypeStruct(block, bf16)] * 2,
        in_specs=whole(3),
        out_specs=whole(2),
        scratch_shapes=[VMEM((pair_count, a_local, LANES), f32)],
        compiler_params=params(),
        name="pack_tiles",
    )(amps, source, mask)
    sem = pltpu.SemaphoreType.DMA
    ring_sems = sem((2, share, 2, col_count // 2))
    partial = pl.pallas_call(
        ladder_kernel,
        out_shape=jax.ShapeDtypeStruct((row_count, slots, virt, a_local), bf16),
        in_specs=[pl.BlockSpec(memory_space=VMEM), pl.BlockSpec(memory_space=pl.ANY)],
        out_specs=pl.BlockSpec(memory_space=VMEM),
        scratch_shapes=[
            VMEM((row_count, slots, row_count, col_count, group, a_local), bf16),
            VMEM((share, row_count, col_count, group, virt), bf16),
            VMEM((virt, virt), bf16),
            VMEM((slots, virt, virt), f32),
            sem((share + 1,)),
            sem((share, row_count - 1)),
            sem((share, row_count - 1)),
            sem((col_count - 1,)),
            sem((col_count - 1,)),
            sem((3,)),
            sem((3,)),
            ring_sems,
            ring_sems,
        ],
        compiler_params=pltpu.CompilerParams(
            vmem_limit_bytes=56 * 1024 * 1024, collective_id=0, has_side_effects=True
        ),
        cost_estimate=pl.CostEstimate(
            flops=4 * share * slots * virt**3, bytes_accessed=16 * 1024 * 1024, transcendentals=0
        ),
        name="ladder",
    )(tm_blocks, factors.reshape(row_count, share, group, virt))
    s_mine = lax.all_to_all(s_blocks, "col", split_axis=0, concat_axis=0, tiled=True)

    ladder = lax.psum_scatter(partial, "row", scatter_dimension=0, tiled=True)
    ladder = ladder.reshape(slots, virt, a_local)
    resid, swap = pl.pallas_call(
        resid_kernel,
        out_shape=[
            jax.ShapeDtypeStruct((slots, virt, a_local), f32),
            jax.ShapeDtypeStruct((row_count, slots, a_local, a_local), bf16),
        ],
        in_specs=whole(2),
        out_specs=whole(2),
        compiler_params=params(),
        name="resid",
    )(ladder, s_mine)
    swapped = lax.all_to_all(swap, "row", split_axis=0, concat_axis=0, tiled=True)
    rsym = pl.pallas_call(
        functools.partial(add_kernel, occ_count * (occ_count - 1) // 2),
        out_shape=jax.ShapeDtypeStruct(block, bf16),
        in_specs=whole(2),
        out_specs=whole(1)[0],
        compiler_params=params(),
        name="add_swapped",
    )(resid, swapped)
    rsym = lax.all_to_all(rsym, "col", split_axis=0, concat_axis=0, tiled=True)
    new = pl.pallas_call(
        functools.partial(update_kernel, table),
        out_shape=jax.ShapeDtypeStruct((pair_count, a_local * b_local), bf16),
        in_specs=whole(5) + [pl.BlockSpec(memory_space=pltpu.SMEM)],
        out_specs=whole(1)[0],
        scratch_shapes=[VMEM((pair_count, a_local, LANES), f32)],
        compiler_params=params(),
        name="update",
    )(amps, rsym, mask, occ_pair, vir_b, vir_a)
    return new.reshape(1, 1, pair_count, a_local * b_local)


def to_col_major(array, dim, row_count, col_count):
    old_shape = array.shape
    group_len = old_shape[dim] // (row_count * col_count)
    divided = array.reshape(
        old_shape[:dim] + (row_count, col_count, group_len) + old_shape[dim + 1 :]
    )
    return jnp.swapaxes(divided, dim, dim + 1).reshape(old_shape)


def ladder_over_aux(running, segment, left_part, right_factor):

    def step(total, factor_pair):
        left_one, right_one = factor_pair
        inner_part = jnp.einsum(
            "pcd,bd->pcb", segment, right_one, preferred_element_type=jnp.float32
        ).astype(jnp.bfloat16)
        return (
            total
            + jnp.einsum("ac,pcb->pab", left_one, inner_part, preferred_element_type=jnp.float32),
            None,
        )

    result, unused = lax.scan(step, running, (left_part, right_factor))
    return result


def shards(amps, source, factors, screen, occ_energy, vir_energy):
    row_count = lax.axis_size("row")
    col_count = lax.axis_size("col")
    row_id = lax.axis_index("row")
    col_id = lax.axis_index("col")
    pair_count = amps.shape[2]
    aux_count, group_size, virt_count = factors.shape
    a_local = col_count * group_size
    b_local = row_count * group_size
    occ_count = occ_energy.shape[0]
    block_count = screen.shape[1]
    block_size = virt_count // block_count
    a_index = row_id * a_local + jnp.arange(a_local)
    b_position = jnp.arange(b_local)
    b_index = b_position // group_size * a_local + col_id * group_size + b_position % group_size
    block_ids = jnp.arange(block_count)
    select_rows = (a_index[:, None] // block_size == block_ids[None, :]).astype(jnp.float32)
    select_cols = (b_index[:, None] // block_size == block_ids[None, :]).astype(jnp.float32)
    mask_tile = jnp.einsum("pxy,ax,by->pab", screen.astype(jnp.float32), select_rows, select_cols)
    amp_tile = amps.reshape(pair_count, a_local, b_local)
    masked = (amp_tile * mask_tile).astype(jnp.bfloat16)
    share_rows = lax.all_to_all(factors, "row", split_axis=0, concat_axis=1, tiled=True)
    col_ordered = lax.all_gather(share_rows, "col", axis=1, tiled=True)
    left_factor = to_col_major(col_ordered, 1, col_count, row_count)
    right_factor = to_col_major(col_ordered, 2, row_count, col_count)
    mine = lax.all_to_all(masked, "col", split_axis=0, concat_axis=2, tiled=True)
    initial = jnp.zeros((mine.shape[0], virt_count, virt_count), jnp.float32)
    ladder_sum = ladder_over_aux(
        initial, lax.all_gather(mine, "row", axis=1, tiled=True), left_factor, right_factor
    )
    reduced = lax.psum_scatter(
        ladder_sum.astype(jnp.bfloat16), "row", scatter_dimension=1, tiled=True
    ).astype(jnp.float32)
    ladder = lax.all_to_all(
        reduced.astype(jnp.bfloat16), "col", split_axis=2, concat_axis=0, tiled=True
    ).astype(reduced.dtype)
    resid = source.reshape(pair_count, a_local, b_local).astype(jnp.float32) + ladder
    split_tile = resid.reshape(pair_count, col_count, group_size, row_count, group_size)
    received = lax.all_to_all(
        lax.all_to_all(
            split_tile.astype(jnp.bfloat16), "row", split_axis=3, concat_axis=3, tiled=True
        ),
        "col",
        split_axis=1,
        concat_axis=1,
        tiled=True,
    ).astype(split_tile.dtype)
    swapped = received.transpose(0, 1, 4, 3, 2).reshape(occ_count, occ_count, a_local, b_local)
    swapped = swapped.transpose(1, 0, 2, 3).reshape(pair_count, a_local, b_local)
    rsym = resid + swapped
    occ_pair = (occ_energy[:, None] + occ_energy[None, :]).reshape(pair_count)
    vir_rows = lax.dynamic_slice_in_dim(vir_energy, row_id * a_local, a_local)
    vir_cols = lax.dynamic_slice_in_dim(
        vir_energy.reshape(row_count, col_count, group_size), col_id, 1, 1
    ).reshape(b_local)
    denominator = occ_pair[:, None, None] - vir_rows[None, :, None] - vir_cols[None, None, :]
    updated = mask_tile * (amp_tile.astype(jnp.float32) + rsym / denominator)
    return updated.astype(jnp.bfloat16).reshape(1, 1, pair_count, a_local * b_local)


def fits(amps, factors, screen, occ_energy, row_count, col_count):
    aux_count, rows, virt = factors.shape
    group = rows // (row_count * col_count)
    a_local, b_local = col_count * group, row_count * group
    block_size = virt // screen.shape[1]
    occ_count = occ_energy.shape[0]
    return (
        group % 16 == 0
        and b_local == LANES
        and a_local % LANES == 0
        and block_size % group == 0
        and a_local % block_size == 0
        and occ_count % 2 == 0
        and 2 * col_count == occ_count * occ_count
        and amps.shape[2] == occ_count * occ_count
        and aux_count % row_count == 0
        and aux_count >= 2 * row_count
        and row_count == 4
        and virt % 512 == 0
        and 512 % a_local == 0
    )


def solution(mesh):
    in_specs = (
        P("row", "col", None, None),
        P("row", "col", None, None),
        P(None, ("row", "col"), None),
        P(),
        P(),
        P(),
    )
    out_specs = P("row", "col", None, None)
    row_count, col_count = mesh.shape["row"], mesh.shape["col"]

    def run(amps, source, factors, screen, occ_energy, vir_energy):
        fast = fits(amps, factors, screen, occ_energy, row_count, col_count)
        body = fast_shards if fast else shards
        return jax.shard_map(
            body, mesh=mesh, in_specs=in_specs, out_specs=out_specs, check_vma=False
        )(amps, source, factors, screen, occ_energy, vir_energy)

    return run
```

```python
import functools

import jax
import jax.numpy as jnp
from jax import lax
from jax.experimental import pallas as pl
from jax.experimental.pallas import tpu as pltpu
from jax.sharding import PartitionSpec as P

VMEM = pltpu.VMEM
LANES = 128


def pair_table(occ_count):
    table = []
    for i in range(occ_count):
        for j in range(i + 1, occ_count):
            table.append((i * occ_count + j, j * occ_count + i))
    for i in range(0, occ_count, 2):
        table.append((i * occ_count + i, (i + 1) * occ_count + i + 1))
    return table


def whole(count):
    return [pl.BlockSpec(memory_space=VMEM)] * count


def pack_kernel(table, amps_ref, source_ref, mask_ref, tm_ref, s_ref, rows):
    pair_count, a_local = rows.shape[0], rows.shape[1]
    groups, group = tm_ref.shape[2], tm_ref.shape[3]
    half_len = a_local // mask_ref.shape[0]

    def turn(in_ref, out_ref, masked):
        for half in range(mask_ref.shape[0]):

            @pl.loop(0, half_len, unroll=8)
            def _(step):
                x = half * half_len + step
                one = in_ref[:, pl.ds(pl.multiple_of(x * LANES, LANES), LANES)].astype(jnp.float32)
                if masked:
                    one = one * mask_ref[half]
                rows[:, x, :] = one

        for dest, pairs in enumerate(table):
            for slot, pair in enumerate(pairs):
                turned = rows[pair].T.astype(jnp.bfloat16)
                out_ref[dest, slot] = turned.reshape(groups, group, a_local)

    turn(amps_ref, tm_ref, True)
    turn(source_ref, s_ref, False)


def ring_column(position, count):
    position = (position + count) % count
    back = position // (count // 2)
    return (1 - back) * 2 * position + back * (2 * (count - 1 - position) + 1)


def ladder_kernel(
    tm_ref,
    factors_ref,
    out_ref,
    t_all,
    b_all,
    inner,
    total,
    near_sem,
    share_send,
    share_recv,
    tile_send,
    tile_recv,
    slab_send,
    slab_recv,
    ring_send,
    ring_recv,
):
    q_count, row_count, col_count, group, virt = b_all.shape
    slots, a_local = t_all.shape[1], t_all.shape[5]
    row, col = lax.axis_index("row"), lax.axis_index("col")
    sibling = row + 1 - 2 * (row % 2)
    across = (row + 2) % row_count
    place = (col // 2) * (1 - col % 2) + (col_count - 1 - col // 2) * (col % 2)
    half_rows = row_count // 2

    def remote(source, dest, send_sem, recv_sem, device):
        return pltpu.make_async_remote_copy(
            src_ref=source,
            dst_ref=dest,
            send_sem=send_sem,
            recv_sem=recv_sem,
            device_id=device,
            device_id_type=pl.DeviceIdType.MESH,
        )

    barrier = pltpu.get_barrier_semaphore()
    for step in range(1, row_count):
        pl.semaphore_signal(
            barrier,
            inc=1,
            device_id={"row": (row + step) % row_count},
            device_id_type=pl.DeviceIdType.MESH,
        )
    for step in range(1, col_count):
        pl.semaphore_signal(
            barrier,
            inc=1,
            device_id={"col": (col + step) % col_count},
            device_id_type=pl.DeviceIdType.MESH,
        )
    pl.semaphore_wait(barrier, row_count + col_count - 2)

    def share_copy(q, step):
        to_row = (row + step) % row_count
        return remote(
            factors_ref.at[to_row, q],
            b_all.at[q, row, col],
            share_send.at[q, step - 1],
            share_recv.at[q, step - 1],
            {"row": to_row},
        )

    def share_arrival(q, step):
        from_row = (row + row_count - step) % row_count
        here = b_all.at[q, from_row, col]
        return remote(here, here, share_send.at[q, step - 1], share_recv.at[q, step - 1], {"row": from_row})

    def tile_copy(step):
        to_col = (col + step) % col_count
        return remote(
            tm_ref.at[to_col],
            t_all.at[row, :, :, col],
            tile_send.at[step - 1],
            tile_recv.at[step - 1],
            {"col": to_col},
        )

    def tile_arrival(step):
        from_col = (col + col_count - step) % col_count
        here = t_all.at[row, :, :, from_col]
        return remote(here, here, tile_send.at[step - 1], tile_recv.at[step - 1], {"col": from_col})

    def slab_copy(kind):
        slab = t_all.at[(row, row, across)[kind]]
        to_row = (sibling, across, sibling)[kind]
        return remote(slab, slab, slab_send.at[kind], slab_recv.at[kind], {"row": to_row})

    def slab_arrival(kind):
        slab = t_all.at[(sibling, across, (sibling + 2) % row_count)[kind]]
        return remote(slab, slab, slab_send.at[kind], slab_recv.at[kind], {"row": sibling})

    def hops(q, way):
        return col_count // 2 - (q + way) % 2

    def ring_block(q, half, position):
        return b_all.at[q, pl.ds(half * half_rows, half_rows), ring_column(position, col_count)]

    def ring_copy(way, q, half, hop):
        sign = 1 - 2 * way
        block = ring_block(q, half, place - sign * hop)
        to_col = ring_column(place + sign, col_count)
        sems = ring_send.at[way, q, half, hop], ring_recv.at[way, q, half, hop]
        return remote(block, block, *sems, {"col": to_col})

    def ring_arrival(way, q, half, hop):
        sign = 1 - 2 * way
        block = ring_block(q, half, place - sign * (hop + 1))
        to_col = ring_column(place + sign, col_count)
        sems = ring_send.at[way, q, half, hop], ring_recv.at[way, q, half, hop]
        return remote(block, block, *sems, {"col": to_col})

    def ring_begin(q):
        for step in range(1, row_count):
            share_arrival(q, step).wait_recv()
        near_share[q].wait()
        for half in range(2):
            for way in range(2):
                ring_copy(way, q, half, 0).start()

    def ring_step(q, hop):
        for half in range(2):
            for way in range(2):
                if hop < hops(q, way):
                    ring_arrival(way, q, half, hop).wait_recv()
                    if hop + 1 < hops(q, way):
                        ring_copy(way, q, half, hop + 1).start()

    near_share = [
        pltpu.make_async_copy(factors_ref.at[row, q], b_all.at[q, row, col], near_sem.at[q])
        for q in range(q_count)
    ]
    near_tile = pltpu.make_async_copy(
        tm_ref.at[col], t_all.at[row, :, :, col], near_sem.at[q_count]
    )
    for q in range(q_count):
        near_share[q].start()
        for step in range(1, row_count):
            share_copy(q, step).start()
    near_tile.start()
    for step in range(1, col_count):
        tile_copy(step).start()

    block = 512
    blocks = virt // block
    rows_per = block // a_local
    stagger = col_count // 4

    def ring_slot(slot):
        q = slot // stagger
        if (slot + 1) % stagger == 0 and q + 1 < q_count:
            ring_begin(q + 1)
        if q < q_count:
            ring_step(q, slot % stagger)
        if q > 0:
            ring_step(q - 1, stagger + slot % stagger)

    ring_begin(0)
    ring_slot(0)
    for step in range(1, col_count):
        tile_arrival(step).wait_recv()
    near_tile.wait()
    slab_copy(0).start()
    slab_copy(1).start()
    for slot in range(1, stagger):
        ring_slot(slot)
    slab_arrival(1).wait_recv()
    slab_copy(2).start()
    for slot in range(stagger, 2 * stagger):
        ring_slot(slot)
    slab_arrival(0).wait_recv()
    slab_arrival(2).wait_recv()

    for q in range(q_count):
        for p in range(slots):

            @pl.loop(0, blocks * row_count)
            def _(step):
                m, n = step // row_count, step % row_count
                left = b_all[q, pl.ds(m * rows_per, rows_per)].reshape(block, virt)
                right = t_all[n, p].reshape(virt, a_local)
                inner[
                    pl.ds(pl.multiple_of(m * block, block), block),
                    pl.ds(pl.multiple_of(n * a_local, a_local), a_local),
                ] = jnp.dot(left, right, preferred_element_type=jnp.float32).astype(jnp.bfloat16)

            @pl.loop(0, blocks * blocks)
            def _(step):
                m, n = step // blocks, step % blocks
                some = pl.ds(pl.multiple_of(m * block, block), block)
                cols = pl.ds(pl.multiple_of(n * block, block), block)
                right = b_all[q, pl.ds(n * rows_per, rows_per)].reshape(block, virt)
                part = lax.dot_general(
                    inner[some, :],
                    right,
                    (((1,), (1,)), ((), ())),
                    preferred_element_type=jnp.float32,
                )
                if q > 0:
                    part = part + total[p, some, cols]
                if q == q_count - 1:
                    for k in range(rows_per):
                        out_ref[n * rows_per + k, p, some, :] = part[
                            :, k * a_local : (k + 1) * a_local
                        ].astype(jnp.bfloat16)
                else:
                    total[p, some, cols] = part

            if q + 1 < q_count:
                for slot in range(p * stagger // slots, (p + 1) * stagger // slots):
                    ring_slot((q + 2) * stagger + slot)

    for q in range(q_count):
        for step in range(1, row_count):
            share_copy(q, step).wait_send()
        for half in range(2):
            for way in range(2):
                for hop in range(hops(q, way)):
                    ring_copy(way, q, half, hop).wait_send()
    for step in range(1, col_count):
        tile_copy(step).wait_send()
    for kind in range(3):
        slab_copy(kind).wait_send()


def resid_kernel(ladder_ref, s_ref, resid_ref, swap_ref):
    col_count, slots, row_count, group, a_local = s_ref.shape
    for p in range(slots):
        for y in range(row_count):
            for c in range(col_count):
                some = pl.ds(y * a_local + c * group, group)
                resid_ref[p, some, :] = s_ref[c, p, y].astype(jnp.float32) + ladder_ref[
                    p, some, :
                ].astype(jnp.float32)
            swap_ref[y, p] = resid_ref[p, pl.ds(y * a_local, a_local), :].T.astype(jnp.bfloat16)


def add_kernel(diagonal_from, resid_ref, swap_ref, out_ref):
    col_count, slots, row_count, group, a_local = out_ref.shape
    flip = (lax.axis_index("col") < diagonal_from).astype(jnp.int32)
    for p in range(slots):
        partner = p * (1 - flip) + (slots - 1 - p) * flip
        for y in range(row_count):
            for c in range(col_count):
                some = pl.ds(y * a_local + c * group, group)
                other = swap_ref[y, partner, pl.ds(c * group, group), :]
                both = resid_ref[p, some, :] + other.astype(jnp.float32)
                out_ref[c, p, y] = both.astype(jnp.bfloat16)


def update_kernel(table, amps_ref, rsym_ref, mask_ref, occ_ref, vir_b_ref, vir_a_ref, out_ref, rows):
    pair_count, a_local = rows.shape[0], rows.shape[1]
    half_len = a_local // mask_ref.shape[0]
    for owner, pairs in enumerate(table):
        for slot, pair in enumerate(pairs):
            one = rsym_ref[owner, slot].reshape(LANES, a_local).astype(jnp.float32)
            rows[pair] = one.T
    known = occ_ref[...] - vir_b_ref[...]
    for half in range(mask_ref.shape[0]):

        @pl.loop(0, half_len, unroll=8)
        def _(step):
            x = half * half_len + step
            lanes = pl.ds(pl.multiple_of(x * LANES, LANES), LANES)
            denom = known - vir_a_ref[x]
            new = mask_ref[half] * (amps_ref[:, lanes].astype(jnp.float32) + rows[:, x, :] / denom)
            out_ref[:, lanes] = new.astype(jnp.bfloat16)


def params(limit=56):
    return pltpu.CompilerParams(vmem_limit_bytes=limit * 1024 * 1024)


def fast_shards(amps, source, factors, screen, occ_energy, vir_energy):
    row_count = lax.axis_size("row")
    col_count = lax.axis_size("col")
    row_id = lax.axis_index("row")
    col_id = lax.axis_index("col")
    pair_count = amps.shape[2]
    aux_count, group, virt = factors.shape
    a_local = col_count * group
    b_local = row_count * group
    occ_count = occ_energy.shape[0]
    block_count = screen.shape[1]
    block_size = virt // block_count
    halves = a_local // block_size
    per_y = block_count // row_count
    slots = pair_count // col_count
    share = aux_count // row_count
    table = pair_table(occ_count)
    bf16, f32 = jnp.bfloat16, jnp.float32

    amps = amps.reshape(pair_count, a_local * b_local)
    source = source.reshape(pair_count, a_local * b_local)
    mine = lax.dynamic_slice_in_dim(screen, row_id * halves, halves, 1)
    mine = mine.reshape(pair_count, halves, row_count, per_y)
    mine = lax.dynamic_slice_in_dim(mine, col_id * group // block_size, 1, 3)
    mask = jnp.broadcast_to(
        mine.transpose(1, 0, 2, 3).astype(f32), (halves, pair_count, row_count, group)
    ).reshape(halves, pair_count, b_local)
    occ_pair = (occ_energy[:, None] + occ_energy[None, :]).reshape(pair_count, 1)
    vir_a = lax.dynamic_slice_in_dim(vir_energy, row_id * a_local, a_local)
    vir_b = lax.dynamic_slice_in_dim(
        vir_energy.reshape(row_count, col_count, group), col_id, 1, 1
    ).reshape(1, b_local)

    block = (col_count, slots, row_count, group, a_local)
    tm_blocks, s_blocks = pl.pallas_call(
        functools.partial(pack_kernel, table),
        out_shape=[jax.ShapeDtypeStruct(block, bf16)] * 2,
        in_specs=whole(3),
        out_specs=whole(2),
        scratch_shapes=[VMEM((pair_count, a_local, LANES), f32)],
        compiler_params=params(),
        name="pack_tiles",
    )(amps, source, mask)
    sem = pltpu.SemaphoreType.DMA
    ring_sems = sem((2, share, 2, col_count // 2))
    partial = pl.pallas_call(
        ladder_kernel,
        out_shape=jax.ShapeDtypeStruct((row_count, slots, virt, a_local), bf16),
        in_specs=[pl.BlockSpec(memory_space=VMEM), pl.BlockSpec(memory_space=pl.ANY)],
        out_specs=pl.BlockSpec(memory_space=VMEM),
        scratch_shapes=[
            VMEM((row_count, slots, row_count, col_count, group, a_local), bf16),
            VMEM((share, row_count, col_count, group, virt), bf16),
            VMEM((virt, virt), bf16),
            VMEM((slots, virt, virt), f32),
            sem((share + 1,)),
            sem((share, row_count - 1)),
            sem((share, row_count - 1)),
            sem((col_count - 1,)),
            sem((col_count - 1,)),
            sem((3,)),
            sem((3,)),
            ring_sems,
            ring_sems,
        ],
        compiler_params=pltpu.CompilerParams(
            vmem_limit_bytes=56 * 1024 * 1024, collective_id=0, has_side_effects=True
        ),
        cost_estimate=pl.CostEstimate(
            flops=4 * share * slots * virt**3, bytes_accessed=16 * 1024 * 1024, transcendentals=0
        ),
        name="ladder",
    )(tm_blocks, factors.reshape(row_count, share, group, virt))
    s_mine = lax.all_to_all(s_blocks, "col", split_axis=0, concat_axis=0, tiled=True)

    ladder = lax.psum_scatter(partial, "row", scatter_dimension=0, tiled=True)
    ladder = ladder.reshape(slots, virt, a_local)
    resid, swap = pl.pallas_call(
        resid_kernel,
        out_shape=[
            jax.ShapeDtypeStruct((slots, virt, a_local), f32),
            jax.ShapeDtypeStruct((row_count, slots, a_local, a_local), bf16),
        ],
        in_specs=whole(2),
        out_specs=whole(2),
        compiler_params=params(),
        name="resid",
    )(ladder, s_mine)
    swapped = lax.all_to_all(swap, "row", split_axis=0, concat_axis=0, tiled=True)
    rsym = pl.pallas_call(
        functools.partial(add_kernel, occ_count * (occ_count - 1) // 2),
        out_shape=jax.ShapeDtypeStruct(block, bf16),
        in_specs=whole(2),
        out_specs=whole(1)[0],
        compiler_params=params(),
        name="add_swapped",
    )(resid, swapped)
    rsym = lax.all_to_all(rsym, "col", split_axis=0, concat_axis=0, tiled=True)
    new = pl.pallas_call(
        functools.partial(update_kernel, table),
        out_shape=jax.ShapeDtypeStruct((pair_count, a_local * b_local), bf16),
        in_specs=whole(5) + [pl.BlockSpec(memory_space=pltpu.SMEM)],
        out_specs=whole(1)[0],
        scratch_shapes=[VMEM((pair_count, a_local, LANES), f32)],
        compiler_params=params(),
        name="update",
    )(amps, rsym, mask, occ_pair, vir_b, vir_a)
    return new.reshape(1, 1, pair_count, a_local * b_local)


def to_col_major(array, dim, row_count, col_count):
    old_shape = array.shape
    group_len = old_shape[dim] // (row_count * col_count)
    divided = array.reshape(
        old_shape[:dim] + (row_count, col_count, group_len) + old_shape[dim + 1 :]
    )
    return jnp.swapaxes(divided, dim, dim + 1).reshape(old_shape)


def ladder_over_aux(running, segment, left_part, right_factor):

    def step(total, factor_pair):
        left_one, right_one = factor_pair
        inner_part = jnp.einsum(
            "pcd,bd->pcb", segment, right_one, preferred_element_type=jnp.float32
        ).astype(jnp.bfloat16)
        return (
            total
            + jnp.einsum("ac,pcb->pab", left_one, inner_part, preferred_element_type=jnp.float32),
            None,
        )

    result, unused = lax.scan(step, running, (left_part, right_factor))
    return result


def shards(amps, source, factors, screen, occ_energy, vir_energy):
    row_count = lax.axis_size("row")
    col_count = lax.axis_size("col")
    row_id = lax.axis_index("row")
    col_id = lax.axis_index("col")
    pair_count = amps.shape[2]
    aux_count, group_size, virt_count = factors.shape
    a_local = col_count * group_size
    b_local = row_count * group_size
    occ_count = occ_energy.shape[0]
    block_count = screen.shape[1]
    block_size = virt_count // block_count
    a_index = row_id * a_local + jnp.arange(a_local)
    b_position = jnp.arange(b_local)
    b_index = b_position // group_size * a_local + col_id * group_size + b_position % group_size
    block_ids = jnp.arange(block_count)
    select_rows = (a_index[:, None] // block_size == block_ids[None, :]).astype(jnp.float32)
    select_cols = (b_index[:, None] // block_size == block_ids[None, :]).astype(jnp.float32)
    mask_tile = jnp.einsum("pxy,ax,by->pab", screen.astype(jnp.float32), select_rows, select_cols)
    amp_tile = amps.reshape(pair_count, a_local, b_local)
    masked = (amp_tile * mask_tile).astype(jnp.bfloat16)
    share_rows = lax.all_to_all(factors, "row", split_axis=0, concat_axis=1, tiled=True)
    col_ordered = lax.all_gather(share_rows, "col", axis=1, tiled=True)
    left_factor = to_col_major(col_ordered, 1, col_count, row_count)
    right_factor = to_col_major(col_ordered, 2, row_count, col_count)
    mine = lax.all_to_all(masked, "col", split_axis=0, concat_axis=2, tiled=True)
    initial = jnp.zeros((mine.shape[0], virt_count, virt_count), jnp.float32)
    ladder_sum = ladder_over_aux(
        initial, lax.all_gather(mine, "row", axis=1, tiled=True), left_factor, right_factor
    )
    reduced = lax.psum_scatter(
        ladder_sum.astype(jnp.bfloat16), "row", scatter_dimension=1, tiled=True
    ).astype(jnp.float32)
    ladder = lax.all_to_all(
        reduced.astype(jnp.bfloat16), "col", split_axis=2, concat_axis=0, tiled=True
    ).astype(reduced.dtype)
    resid = source.reshape(pair_count, a_local, b_local).astype(jnp.float32) + ladder
    split_tile = resid.reshape(pair_count, col_count, group_size, row_count, group_size)
    received = lax.all_to_all(
        lax.all_to_all(
            split_tile.astype(jnp.bfloat16), "row", split_axis=3, concat_axis=3, tiled=True
        ),
        "col",
        split_axis=1,
        concat_axis=1,
        tiled=True,
    ).astype(split_tile.dtype)
    swapped = received.transpose(0, 1, 4, 3, 2).reshape(occ_count, occ_count, a_local, b_local)
    swapped = swapped.transpose(1, 0, 2, 3).reshape(pair_count, a_local, b_local)
    rsym = resid + swapped
    occ_pair = (occ_energy[:, None] + occ_energy[None, :]).reshape(pair_count)
    vir_rows = lax.dynamic_slice_in_dim(vir_energy, row_id * a_local, a_local)
    vir_cols = lax.dynamic_slice_in_dim(
        vir_energy.reshape(row_count, col_count, group_size), col_id, 1, 1
    ).reshape(b_local)
    denominator = occ_pair[:, None, None] - vir_rows[None, :, None] - vir_cols[None, None, :]
    updated = mask_tile * (amp_tile.astype(jnp.float32) + rsym / denominator)
    return updated.astype(jnp.bfloat16).reshape(1, 1, pair_count, a_local * b_local)


def fits(amps, factors, screen, occ_energy, row_count, col_count):
    aux_count, rows, virt = factors.shape
    group = rows // (row_count * col_count)
    a_local, b_local = col_count * group, row_count * group
    block_size = virt // screen.shape[1]
    occ_count = occ_energy.shape[0]
    return (
        group % 16 == 0
        and b_local == LANES
        and a_local % LANES == 0
        and block_size % group == 0
        and a_local % block_size == 0
        and occ_count % 2 == 0
        and 2 * col_count == occ_count * occ_count
        and amps.shape[2] == occ_count * occ_count
        and aux_count % row_count == 0
        and aux_count >= 2 * row_count
        and row_count == 4
        and col_count % 4 == 0
        and virt % 512 == 0
        and 512 % a_local == 0
    )


def solution(mesh):
    in_specs = (
        P("row", "col", None, None),
        P("row", "col", None, None),
        P(None, ("row", "col"), None),
        P(),
        P(),
        P(),
    )
    out_specs = P("row", "col", None, None)
    row_count, col_count = mesh.shape["row"], mesh.shape["col"]

    def run(amps, source, factors, screen, occ_energy, vir_energy):
        fast = fits(amps, factors, screen, occ_energy, row_count, col_count)
        body = fast_shards if fast else shards
        return jax.shard_map(
            body, mesh=mesh, in_specs=in_specs, out_specs=out_specs, check_vma=False
        )(amps, source, factors, screen, occ_energy, vir_energy)

    return run
```

```python
import functools

import jax
import jax.numpy as jnp
from jax import lax
from jax.experimental import pallas as pl
from jax.experimental.pallas import tpu as pltpu
from jax.sharding import PartitionSpec as P

VMEM = pltpu.VMEM
LANES = 128


def pair_table(occ_count):
    table = []
    for i in range(occ_count):
        for j in range(i + 1, occ_count):
            table.append((i * occ_count + j, j * occ_count + i))
    for i in range(0, occ_count, 2):
        table.append((i * occ_count + i, (i + 1) * occ_count + i + 1))
    return table


def whole(count):
    return [pl.BlockSpec(memory_space=VMEM)] * count


def pack_kernel(table, amps_ref, source_ref, mask_ref, tm_ref, s_ref, rows):
    pair_count, a_local = rows.shape[0], rows.shape[1]
    groups, group = tm_ref.shape[2], tm_ref.shape[3]
    half_len = a_local // mask_ref.shape[0]

    def turn(in_ref, out_ref, masked):
        for half in range(mask_ref.shape[0]):

            @pl.loop(0, half_len, unroll=8)
            def _(step):
                x = half * half_len + step
                one = in_ref[:, pl.ds(pl.multiple_of(x * LANES, LANES), LANES)].astype(jnp.float32)
                if masked:
                    one = one * mask_ref[half]
                rows[:, x, :] = one

        for dest, pairs in enumerate(table):
            for slot, pair in enumerate(pairs):
                turned = rows[pair].T.astype(jnp.bfloat16)
                out_ref[dest, slot] = turned.reshape(groups, group, a_local)

    turn(amps_ref, tm_ref, True)
    turn(source_ref, s_ref, False)


def ring_column(position, count):
    position = (position + count) % count
    back = position // (count // 2)
    return (1 - back) * 2 * position + back * (2 * (count - 1 - position) + 1)


def ladder_kernel(
    diagonal_from,
    tm_ref,
    s_ref,
    factors_ref,
    out_ref,
    t_all,
    b_all,
    inner,
    total,
    part,
    core_in,
    across_in,
    s_all,
    resid,
    swap_out,
    swap_in,
    rsym,
    near_sem,
    share_send,
    share_recv,
    tile_send,
    tile_recv,
    slab_send,
    slab_recv,
    ring_send,
    ring_recv,
    s_send,
    s_recv,
    core_send,
    core_recv,
    across_send,
    across_recv,
    swap_send,
    swap_recv,
    back_send,
    back_recv,
):
    q_count, row_count, col_count, group, virt = b_all.shape
    slots, a_local = t_all.shape[1], t_all.shape[5]
    row, col = lax.axis_index("row"), lax.axis_index("col")
    sibling = row + 1 - 2 * (row % 2)
    across = (row + 2) % row_count
    diagonal = (sibling + 2) % row_count
    chip = row // 2
    rows_by = (row, sibling, across, diagonal)
    place = (col // 2) * (1 - col % 2) + (col_count - 1 - col // 2) * (col % 2)
    half_rows = row_count // 2

    def remote(source, dest, send_sem, recv_sem, device):
        return pltpu.make_async_remote_copy(
            src_ref=source,
            dst_ref=dest,
            send_sem=send_sem,
            recv_sem=recv_sem,
            device_id=device,
            device_id_type=pl.DeviceIdType.MESH,
        )

    barrier = pltpu.get_barrier_semaphore()
    for step in range(1, row_count):
        pl.semaphore_signal(
            barrier,
            inc=1,
            device_id={"row": (row + step) % row_count},
            device_id_type=pl.DeviceIdType.MESH,
        )
    for step in range(1, col_count):
        pl.semaphore_signal(
            barrier,
            inc=1,
            device_id={"col": (col + step) % col_count},
            device_id_type=pl.DeviceIdType.MESH,
        )
    pl.semaphore_wait(barrier, row_count + col_count - 2)

    def share_copy(q, step):
        to_row = (row + step) % row_count
        return remote(
            factors_ref.at[to_row, q],
            b_all.at[q, row, col],
            share_send.at[q, step - 1],
            share_recv.at[q, step - 1],
            {"row": to_row},
        )

    def share_arrival(q, step):
        from_row = (row + row_count - step) % row_count
        here = b_all.at[q, from_row, col]
        return remote(here, here, share_send.at[q, step - 1], share_recv.at[q, step - 1], {"row": from_row})

    def tile_copy(step):
        to_col = (col + step) % col_count
        return remote(
            tm_ref.at[to_col],
            t_all.at[row, :, :, col],
            tile_send.at[step - 1],
            tile_recv.at[step - 1],
            {"col": to_col},
        )

    def tile_arrival(step):
        from_col = (col + col_count - step) % col_count
        here = t_all.at[row, :, :, from_col]
        return remote(here, here, tile_send.at[step - 1], tile_recv.at[step - 1], {"col": from_col})

    def slab_copy(kind, step):
        from_col = (col + col_count - step) % col_count
        slab = t_all.at[(row, row, across)[kind], :, :, from_col]
        to_row = (sibling, across, sibling)[kind]
        sems = slab_send.at[kind, step], slab_recv.at[kind, step]
        return remote(slab, slab, *sems, {"row": to_row})

    def slab_arrival(kind, step):
        from_col = (col + col_count - step) % col_count
        slab = t_all.at[(sibling, across, diagonal)[kind], :, :, from_col]
        sems = slab_send.at[kind, step], slab_recv.at[kind, step]
        return remote(slab, slab, *sems, {"row": sibling})

    def hops(q, way):
        return col_count // 2 - (q + way) % 2

    def ring_block(q, half, position):
        return b_all.at[q, pl.ds(half * half_rows, half_rows), ring_column(position, col_count)]

    def ring_copy(way, q, half, hop):
        sign = 1 - 2 * way
        block = ring_block(q, half, place - sign * hop)
        to_col = ring_column(place + sign, col_count)
        sems = ring_send.at[way, q, half, hop], ring_recv.at[way, q, half, hop]
        return remote(block, block, *sems, {"col": to_col})

    def ring_arrival(way, q, half, hop):
        sign = 1 - 2 * way
        block = ring_block(q, half, place - sign * (hop + 1))
        to_col = ring_column(place + sign, col_count)
        sems = ring_send.at[way, q, half, hop], ring_recv.at[way, q, half, hop]
        return remote(block, block, *sems, {"col": to_col})

    def ring_begin(q):
        for step in range(1, row_count):
            share_arrival(q, step).wait_recv()
        near_share[q].wait()
        for half in range(2):
            for way in range(2):
                ring_copy(way, q, half, 0).start()

    def ring_step(q, hop):
        for half in range(2):
            for way in range(2):
                if hop < hops(q, way):
                    ring_arrival(way, q, half, hop).wait_recv()
                    if hop + 1 < hops(q, way):
                        ring_copy(way, q, half, hop + 1).start()

    def s_copy(step):
        to_col = (col + step) % col_count
        sems = s_send.at[step - 1], s_recv.at[step - 1]
        return remote(s_ref.at[to_col], s_all.at[col], *sems, {"col": to_col})

    def s_arrival(step):
        from_col = (col + col_count - step) % col_count
        here = s_all.at[from_col]
        return remote(here, here, s_send.at[step - 1], s_recv.at[step - 1], {"col": from_col})

    def core_copy(p, near):
        source = part.at[sibling if near else diagonal, p]
        dest = core_in.at[chip if near else 1 - chip, p]
        return remote(source, dest, core_send.at[p, near], core_recv.at[p, near], {"row": sibling})

    def core_arrival(p, near):
        here = core_in.at[chip if near else 1 - chip, p]
        return remote(here, here, core_send.at[p, near], core_recv.at[p, near], {"row": sibling})

    def across_copy(p):
        sems = across_send.at[p], across_recv.at[p]
        return remote(part.at[across, p], across_in.at[p], *sems, {"row": across})

    def across_arrival(p):
        here = across_in.at[p]
        return remote(here, here, across_send.at[p], across_recv.at[p], {"row": across})

    def send_across(p):
        core_arrival(p, 0).wait_recv()

        @pl.loop(0, row_count)
        def _(y):
            some = pl.ds(pl.multiple_of(y * a_local, a_local), a_local)
            both = part[across, p, some, :].astype(jnp.float32) + core_in[
                1 - chip, p, some, :
            ].astype(jnp.float32)
            part[across, p, some, :] = both.astype(jnp.bfloat16)

        across_copy(p).start()

    def swap_copy(kind, p):
        sems = swap_send.at[kind - 1, p], swap_recv.at[kind - 1, p]
        return remote(swap_out.at[kind - 1, p], swap_in.at[row, p], *sems, {"row": rows_by[kind]})

    def swap_arrival(kind, p):
        here = swap_in.at[rows_by[kind], p]
        sems = swap_send.at[kind - 1, p], swap_recv.at[kind - 1, p]
        return remote(here, here, *sems, {"row": rows_by[kind]})

    def back_copy(kind, step):
        to_col = (col + step) % col_count
        sems = back_send.at[kind, step - 1], back_recv.at[kind, step - 1]
        dest = out_ref.at[col, rows_by[kind]]
        return remote(rsym.at[kind, to_col], dest, *sems, {"col": to_col})

    def back_arrival(kind, step):
        from_col = (col + col_count - step) % col_count
        here = out_ref.at[from_col, rows_by[kind]]
        sems = back_send.at[kind, step - 1], back_recv.at[kind, step - 1]
        return remote(here, here, *sems, {"col": from_col})

    near_s = pltpu.make_async_copy(s_ref.at[col], s_all.at[col], near_sem.at[q_count + 1])
    near_share = [
        pltpu.make_async_copy(factors_ref.at[row, q], b_all.at[q, row, col], near_sem.at[q])
        for q in range(q_count)
    ]
    near_tile = pltpu.make_async_copy(
        tm_ref.at[col], t_all.at[row, :, :, col], near_sem.at[q_count]
    )
    near_tile.start()
    for step in range(1, col_count):
        tile_copy(step).start()
    for q in range(q_count):
        near_share[q].start()
        for step in range(1, row_count):
            share_copy(q, step).start()

    block = 512
    blocks = virt // block
    rows_per = block // a_local
    stagger = col_count // 4

    def ring_slot(slot):
        q = slot // stagger
        if (slot + 1) % stagger == 0 and q + 1 < q_count:
            ring_begin(q + 1)
        if q < q_count:
            ring_step(q, slot % stagger)
        if q > 0:
            ring_step(q - 1, stagger + slot % stagger)

    near_tile.wait()
    slab_copy(0, 0).start()
    slab_copy(1, 0).start()
    ring_begin(0)
    for step in range(1, col_count):
        tile_arrival(step).wait_recv()
        slab_copy(0, step).start()
        slab_copy(1, step).start()
    for slot in range(stagger):
        ring_slot(slot)
    for step in range(col_count):
        slab_arrival(1, step).wait_recv()
        slab_copy(2, step).start()
    for slot in range(stagger, 2 * stagger):
        ring_slot(slot)
    for step in range(col_count):
        slab_arrival(0, step).wait_recv()
        slab_arrival(2, step).wait_recv()

    for q in range(q_count):
        if q == q_count - 1:
            near_s.start()
            for step in range(1, col_count):
                s_copy(step).start()
        for p in range(slots):

            @pl.loop(0, blocks * row_count)
            def _(step):
                m, n = step // row_count, step % row_count
                left = b_all[q, pl.ds(m * rows_per, rows_per)].reshape(block, virt)
                right = t_all[n, p].reshape(virt, a_local)
                inner[
                    pl.ds(pl.multiple_of(m * block, block), block),
                    pl.ds(pl.multiple_of(n * a_local, a_local), a_local),
                ] = jnp.dot(left, right, preferred_element_type=jnp.float32).astype(jnp.bfloat16)

            if q == q_count - 1 and p > 0:
                send_across(p - 1)

            @pl.loop(0, blocks * blocks)
            def _(step):
                m, n = step // blocks, step % blocks
                some = pl.ds(pl.multiple_of(m * block, block), block)
                cols = pl.ds(pl.multiple_of(n * block, block), block)
                right = b_all[q, pl.ds(n * rows_per, rows_per)].reshape(block, virt)
                product = lax.dot_general(
                    inner[some, :],
                    right,
                    (((1,), (1,)), ((), ())),
                    preferred_element_type=jnp.float32,
                )
                if q > 0:
                    product = product + total[p, some, cols]
                if q == q_count - 1:
                    for k in range(rows_per):
                        part[n * rows_per + k, p, some, :] = product[
                            :, k * a_local : (k + 1) * a_local
                        ].astype(jnp.bfloat16)
                else:
                    total[p, some, cols] = product

            if q + 1 < q_count:
                for slot in range(p * stagger // slots, (p + 1) * stagger // slots):
                    ring_slot((q + 2) * stagger + slot)
            else:
                core_copy(p, 0).start()
                core_copy(p, 1).start()

    send_across(slots - 1)
    near_s.wait()
    for step in range(1, col_count):
        s_arrival(step).wait_recv()

    for p in range(slots):
        core_arrival(p, 1).wait_recv()
        across_arrival(p).wait_recv()
        for y in range(row_count):
            for c in range(col_count):
                some = pl.ds(y * a_local + c * group, group)
                resid[p, some, :] = (
                    part[row, p, some, :].astype(jnp.float32)
                    + core_in[chip, p, some, :].astype(jnp.float32)
                    + across_in[p, some, :].astype(jnp.float32)
                    + s_all[c, p, y].astype(jnp.float32)
                )
        for kind in range(row_count - 1, -1, -1):
            some = pl.ds(pl.multiple_of(rows_by[kind] * a_local, a_local), a_local)
            turned = resid[p, some, :].T.astype(jnp.bfloat16)
            if kind == 0:
                swap_in[row, p] = turned
            else:
                swap_out[kind - 1, p] = turned
                swap_copy(kind, p).start()

    flip = 1 - (col + col_count - diagonal_from) // col_count
    for kind in range(row_count):
        y = rows_by[kind]
        if kind > 0:
            for p in range(slots):
                swap_arrival(kind, p).wait_recv()
        for p in range(slots):
            partner = p * (1 - flip) + (slots - 1 - p) * flip
            for c in range(col_count):
                some = pl.ds(pl.multiple_of(y * a_local + c * group, group), group)
                other = swap_in[y, partner, pl.ds(c * group, group), :]
                both = resid[p, some, :] + other.astype(jnp.float32)
                rsym[kind, c, p] = both.astype(jnp.bfloat16)
        for step in range(1, col_count):
            back_copy(kind, step).start()
        out_ref[col, y] = rsym[kind, col]
    for kind in range(row_count):
        for step in range(1, col_count):
            back_arrival(kind, step).wait_recv()

    for q in range(q_count):
        for step in range(1, row_count):
            share_copy(q, step).wait_send()
        for half in range(2):
            for way in range(2):
                for hop in range(hops(q, way)):
                    ring_copy(way, q, half, hop).wait_send()
    for step in range(1, col_count):
        tile_copy(step).wait_send()
        s_copy(step).wait_send()
        for kind in range(row_count):
            back_copy(kind, step).wait_send()
    for kind in range(3):
        for step in range(col_count):
            slab_copy(kind, step).wait_send()
        for p in range(slots):
            swap_copy(kind + 1, p).wait_send()
    for p in range(slots):
        core_copy(p, 0).wait_send()
        core_copy(p, 1).wait_send()
        across_copy(p).wait_send()


def update_kernel(table, amps_ref, rsym_ref, mask_ref, occ_ref, vir_b_ref, vir_a_ref, out_ref, rows):
    pair_count, a_local = rows.shape[0], rows.shape[1]
    half_len = a_local // mask_ref.shape[0]
    for owner, pairs in enumerate(table):
        for slot, pair in enumerate(pairs):
            one = rsym_ref[owner, :, slot].reshape(LANES, a_local).astype(jnp.float32)
            rows[pair] = one.T
    known = occ_ref[...] - vir_b_ref[...]
    for half in range(mask_ref.shape[0]):

        @pl.loop(0, half_len, unroll=8)
        def _(step):
            x = half * half_len + step
            lanes = pl.ds(pl.multiple_of(x * LANES, LANES), LANES)
            denom = known - vir_a_ref[x]
            new = mask_ref[half] * (amps_ref[:, lanes].astype(jnp.float32) + rows[:, x, :] / denom)
            out_ref[:, lanes] = new.astype(jnp.bfloat16)


def params(limit=56):
    return pltpu.CompilerParams(vmem_limit_bytes=limit * 1024 * 1024)


def fast_shards(amps, source, factors, screen, occ_energy, vir_energy):
    row_count = lax.axis_size("row")
    col_count = lax.axis_size("col")
    row_id = lax.axis_index("row")
    col_id = lax.axis_index("col")
    pair_count = amps.shape[2]
    aux_count, group, virt = factors.shape
    a_local = col_count * group
    b_local = row_count * group
    occ_count = occ_energy.shape[0]
    block_count = screen.shape[1]
    block_size = virt // block_count
    halves = a_local // block_size
    per_y = block_count // row_count
    slots = pair_count // col_count
    share = aux_count // row_count
    table = pair_table(occ_count)
    bf16, f32 = jnp.bfloat16, jnp.float32

    amps = amps.reshape(pair_count, a_local * b_local)
    source = source.reshape(pair_count, a_local * b_local)
    mine = lax.dynamic_slice_in_dim(screen, row_id * halves, halves, 1)
    mine = mine.reshape(pair_count, halves, row_count, per_y)
    mine = lax.dynamic_slice_in_dim(mine, col_id * group // block_size, 1, 3)
    mask = jnp.broadcast_to(
        mine.transpose(1, 0, 2, 3).astype(f32), (halves, pair_count, row_count, group)
    ).reshape(halves, pair_count, b_local)
    occ_pair = (occ_energy[:, None] + occ_energy[None, :]).reshape(pair_count, 1)
    vir_a = lax.dynamic_slice_in_dim(vir_energy, row_id * a_local, a_local)
    vir_b = lax.dynamic_slice_in_dim(
        vir_energy.reshape(row_count, col_count, group), col_id, 1, 1
    ).reshape(1, b_local)

    block = (col_count, slots, row_count, group, a_local)
    tm_blocks, s_blocks = pl.pallas_call(
        functools.partial(pack_kernel, table),
        out_shape=[jax.ShapeDtypeStruct(block, bf16)] * 2,
        in_specs=whole(3),
        out_specs=whole(2),
        scratch_shapes=[VMEM((pair_count, a_local, LANES), f32)],
        compiler_params=params(),
        name="pack_tiles",
    )(amps, source, mask)
    sem = pltpu.SemaphoreType.DMA
    ring_sems = sem((2, share, 2, col_count // 2))
    back = (col_count, row_count, slots, group, a_local)
    rsym = pl.pallas_call(
        functools.partial(ladder_kernel, occ_count * (occ_count - 1) // 2),
        out_shape=jax.ShapeDtypeStruct(back, bf16),
        in_specs=[pl.BlockSpec(memory_space=VMEM)] + [pl.BlockSpec(memory_space=pl.ANY)] * 2,
        out_specs=pl.BlockSpec(memory_space=VMEM),
        scratch_shapes=[
            VMEM((row_count, slots, row_count, col_count, group, a_local), bf16),
            VMEM((share, row_count, col_count, group, virt), bf16),
            VMEM((virt, virt), bf16),
            VMEM((slots, virt, virt), f32),
            VMEM((row_count, slots, virt, a_local), bf16),
            VMEM((row_count // 2, slots, virt, a_local), bf16),
            VMEM((slots, virt, a_local), bf16),
            VMEM(block, bf16),
            VMEM((slots, virt, a_local), f32),
            VMEM((row_count - 1, slots, a_local, a_local), bf16),
            VMEM((row_count, slots, a_local, a_local), bf16),
            VMEM((row_count, col_count, slots, group, a_local), bf16),
            sem((share + 2,)),
            sem((share, row_count - 1)),
            sem((share, row_count - 1)),
            sem((col_count - 1,)),
            sem((col_count - 1,)),
            sem((3, col_count)),
            sem((3, col_count)),
            ring_sems,
            ring_sems,
            sem((col_count - 1,)),
            sem((col_count - 1,)),
            sem((slots, 2)),
            sem((slots, 2)),
            sem((slots,)),
            sem((slots,)),
            sem((row_count - 1, slots)),
            sem((row_count - 1, slots)),
            sem((row_count, col_count - 1)),
            sem((row_count, col_count - 1)),
        ],
        compiler_params=pltpu.CompilerParams(
            vmem_limit_bytes=56 * 1024 * 1024, collective_id=0, has_side_effects=True
        ),
        cost_estimate=pl.CostEstimate(
            flops=4 * share * slots * virt**3, bytes_accessed=16 * 1024 * 1024, transcendentals=0
        ),
        name="ladder",
    )(tm_blocks, s_blocks, factors.reshape(row_count, share, group, virt))
    new = pl.pallas_call(
        functools.partial(update_kernel, table),
        out_shape=jax.ShapeDtypeStruct((pair_count, a_local * b_local), bf16),
        in_specs=whole(5) + [pl.BlockSpec(memory_space=pltpu.SMEM)],
        out_specs=whole(1)[0],
        scratch_shapes=[VMEM((pair_count, a_local, LANES), f32)],
        compiler_params=params(),
        name="update",
    )(amps, rsym, mask, occ_pair, vir_b, vir_a)
    return new.reshape(1, 1, pair_count, a_local * b_local)


def to_col_major(array, dim, row_count, col_count):
    old_shape = array.shape
    group_len = old_shape[dim] // (row_count * col_count)
    divided = array.reshape(
        old_shape[:dim] + (row_count, col_count, group_len) + old_shape[dim + 1 :]
    )
    return jnp.swapaxes(divided, dim, dim + 1).reshape(old_shape)


def ladder_over_aux(running, segment, left_part, right_factor):

    def step(total, factor_pair):
        left_one, right_one = factor_pair
        inner_part = jnp.einsum(
            "pcd,bd->pcb", segment, right_one, preferred_element_type=jnp.float32
        ).astype(jnp.bfloat16)
        return (
            total
            + jnp.einsum("ac,pcb->pab", left_one, inner_part, preferred_element_type=jnp.float32),
            None,
        )

    result, unused = lax.scan(step, running, (left_part, right_factor))
    return result


def shards(amps, source, factors, screen, occ_energy, vir_energy):
    row_count = lax.axis_size("row")
    col_count = lax.axis_size("col")
    row_id = lax.axis_index("row")
    col_id = lax.axis_index("col")
    pair_count = amps.shape[2]
    aux_count, group_size, virt_count = factors.shape
    a_local = col_count * group_size
    b_local = row_count * group_size
    occ_count = occ_energy.shape[0]
    block_count = screen.shape[1]
    block_size = virt_count // block_count
    a_index = row_id * a_local + jnp.arange(a_local)
    b_position = jnp.arange(b_local)
    b_index = b_position // group_size * a_local + col_id * group_size + b_position % group_size
    block_ids = jnp.arange(block_count)
    select_rows = (a_index[:, None] // block_size == block_ids[None, :]).astype(jnp.float32)
    select_cols = (b_index[:, None] // block_size == block_ids[None, :]).astype(jnp.float32)
    mask_tile = jnp.einsum("pxy,ax,by->pab", screen.astype(jnp.float32), select_rows, select_cols)
    amp_tile = amps.reshape(pair_count, a_local, b_local)
    masked = (amp_tile * mask_tile).astype(jnp.bfloat16)
    share_rows = lax.all_to_all(factors, "row", split_axis=0, concat_axis=1, tiled=True)
    col_ordered = lax.all_gather(share_rows, "col", axis=1, tiled=True)
    left_factor = to_col_major(col_ordered, 1, col_count, row_count)
    right_factor = to_col_major(col_ordered, 2, row_count, col_count)
    mine = lax.all_to_all(masked, "col", split_axis=0, concat_axis=2, tiled=True)
    initial = jnp.zeros((mine.shape[0], virt_count, virt_count), jnp.float32)
    ladder_sum = ladder_over_aux(
        initial, lax.all_gather(mine, "row", axis=1, tiled=True), left_factor, right_factor
    )
    reduced = lax.psum_scatter(
        ladder_sum.astype(jnp.bfloat16), "row", scatter_dimension=1, tiled=True
    ).astype(jnp.float32)
    ladder = lax.all_to_all(
        reduced.astype(jnp.bfloat16), "col", split_axis=2, concat_axis=0, tiled=True
    ).astype(reduced.dtype)
    resid = source.reshape(pair_count, a_local, b_local).astype(jnp.float32) + ladder
    split_tile = resid.reshape(pair_count, col_count, group_size, row_count, group_size)
    received = lax.all_to_all(
        lax.all_to_all(
            split_tile.astype(jnp.bfloat16), "row", split_axis=3, concat_axis=3, tiled=True
        ),
        "col",
        split_axis=1,
        concat_axis=1,
        tiled=True,
    ).astype(split_tile.dtype)
    swapped = received.transpose(0, 1, 4, 3, 2).reshape(occ_count, occ_count, a_local, b_local)
    swapped = swapped.transpose(1, 0, 2, 3).reshape(pair_count, a_local, b_local)
    rsym = resid + swapped
    occ_pair = (occ_energy[:, None] + occ_energy[None, :]).reshape(pair_count)
    vir_rows = lax.dynamic_slice_in_dim(vir_energy, row_id * a_local, a_local)
    vir_cols = lax.dynamic_slice_in_dim(
        vir_energy.reshape(row_count, col_count, group_size), col_id, 1, 1
    ).reshape(b_local)
    denominator = occ_pair[:, None, None] - vir_rows[None, :, None] - vir_cols[None, None, :]
    updated = mask_tile * (amp_tile.astype(jnp.float32) + rsym / denominator)
    return updated.astype(jnp.bfloat16).reshape(1, 1, pair_count, a_local * b_local)


def fits(amps, factors, screen, occ_energy, row_count, col_count):
    aux_count, rows, virt = factors.shape
    group = rows // (row_count * col_count)
    a_local, b_local = col_count * group, row_count * group
    block_size = virt // screen.shape[1]
    occ_count = occ_energy.shape[0]
    return (
        group % 16 == 0
        and b_local == LANES
        and a_local % LANES == 0
        and block_size % group == 0
        and a_local % block_size == 0
        and occ_count % 2 == 0
        and 2 * col_count == occ_count * occ_count
        and amps.shape[2] == occ_count * occ_count
        and aux_count % row_count == 0
        and aux_count >= 2 * row_count
        and row_count == 4
        and col_count % 4 == 0
        and virt % 512 == 0
        and 512 % a_local == 0
    )


def solution(mesh):
    in_specs = (
        P("row", "col", None, None),
        P("row", "col", None, None),
        P(None, ("row", "col"), None),
        P(),
        P(),
        P(),
    )
    out_specs = P("row", "col", None, None)
    row_count, col_count = mesh.shape["row"], mesh.shape["col"]

    def run(amps, source, factors, screen, occ_energy, vir_energy):
        fast = fits(amps, factors, screen, occ_energy, row_count, col_count)
        body = fast_shards if fast else shards
        return jax.shard_map(
            body, mesh=mesh, in_specs=in_specs, out_specs=out_specs, check_vma=False
        )(amps, source, factors, screen, occ_energy, vir_energy)

    return run
```

```python
import functools

import jax
import jax.numpy as jnp
from jax import lax
from jax.experimental import pallas as pl
from jax.experimental.pallas import tpu as pltpu
from jax.sharding import PartitionSpec as P

VMEM = pltpu.VMEM
LANES = 128


def pair_table(occ_count):
    table = []
    for i in range(occ_count):
        for j in range(i + 1, occ_count):
            table.append((i * occ_count + j, j * occ_count + i))
    for i in range(0, occ_count, 2):
        table.append((i * occ_count + i, (i + 1) * occ_count + i + 1))
    return table


def whole(count):
    return [pl.BlockSpec(memory_space=VMEM)] * count


def turn(table, in_ref, out_ref, rows, mask_ref, halves):
    a_local = rows.shape[1]
    groups, group = out_ref.shape[2], out_ref.shape[3]
    half_len = a_local // halves
    for half in range(halves):

        @pl.loop(0, half_len, unroll=8)
        def _(step):
            x = half * half_len + step
            one = in_ref[:, pl.ds(pl.multiple_of(x * LANES, LANES), LANES)].astype(jnp.float32)
            if mask_ref is not None:
                one = one * mask_ref[half]
            rows[:, x, :] = one

    for dest, pairs in enumerate(table):
        for slot, pair in enumerate(pairs):
            turned = rows[pair].T.astype(jnp.bfloat16)
            out_ref[dest, slot] = turned.reshape(groups, group, a_local)


def ring_column(position, count):
    position = (position + count) % count
    back = position // (count // 2)
    return (1 - back) * 2 * position + back * (2 * (count - 1 - position) + 1)


def ladder_kernel(
    table,
    diagonal_from,
    amps_ref,
    source_ref,
    mask_ref,
    factors_ref,
    out_ref,
    rows,
    tm_ref,
    s_ref,
    t_all,
    b_all,
    inner,
    total,
    part,
    core_in,
    across_in,
    s_all,
    resid,
    swap_out,
    swap_in,
    rsym,
    near_sem,
    share_send,
    share_recv,
    tile_send,
    tile_recv,
    slab_send,
    slab_recv,
    ring_send,
    ring_recv,
    s_send,
    s_recv,
    core_send,
    core_recv,
    across_send,
    across_recv,
    swap_send,
    swap_recv,
    back_send,
    back_recv,
):
    q_count, row_count, col_count, group, virt = b_all.shape
    slots, a_local = t_all.shape[1], t_all.shape[5]
    block = 512
    blocks = virt // block
    rows_per = block // a_local
    row, col = lax.axis_index("row"), lax.axis_index("col")
    sibling = row + 1 - 2 * (row % 2)
    across = (row + 2) % row_count
    diagonal = (sibling + 2) % row_count
    chip = row // 2
    rows_by = (row, sibling, across, diagonal)
    place = (col // 2) * (1 - col % 2) + (col_count - 1 - col // 2) * (col % 2)
    half_rows = row_count // 2

    def remote(source, dest, send_sem, recv_sem, device):
        return pltpu.make_async_remote_copy(
            src_ref=source,
            dst_ref=dest,
            send_sem=send_sem,
            recv_sem=recv_sem,
            device_id=device,
            device_id_type=pl.DeviceIdType.MESH,
        )

    barrier = pltpu.get_barrier_semaphore()
    for step in range(1, row_count):
        pl.semaphore_signal(
            barrier,
            inc=1,
            device_id={"row": (row + step) % row_count},
            device_id_type=pl.DeviceIdType.MESH,
        )
    for step in range(1, col_count):
        pl.semaphore_signal(
            barrier,
            inc=1,
            device_id={"col": (col + step) % col_count},
            device_id_type=pl.DeviceIdType.MESH,
        )
    pl.semaphore_wait(barrier, row_count + col_count - 2)

    def share_copy(q, step):
        to_row = (row + step) % row_count
        return remote(
            factors_ref.at[to_row, q],
            b_all.at[q, row, col],
            share_send.at[q, step - 1],
            share_recv.at[q, step - 1],
            {"row": to_row},
        )

    def share_arrival(q, step):
        from_row = (row + row_count - step) % row_count
        here = b_all.at[q, from_row, col]
        return remote(here, here, share_send.at[q, step - 1], share_recv.at[q, step - 1], {"row": from_row})

    def tile_copy(step):
        to_col = (col + step) % col_count
        return remote(
            tm_ref.at[to_col],
            t_all.at[row, :, :, col],
            tile_send.at[step - 1],
            tile_recv.at[step - 1],
            {"col": to_col},
        )

    def tile_arrival(step):
        from_col = (col + col_count - step) % col_count
        here = t_all.at[row, :, :, from_col]
        return remote(here, here, tile_send.at[step - 1], tile_recv.at[step - 1], {"col": from_col})

    def slab_copy(kind, step):
        from_col = (col + col_count - step) % col_count
        slab = t_all.at[(row, row, across)[kind], :, :, from_col]
        to_row = (sibling, across, sibling)[kind]
        sems = slab_send.at[kind, step], slab_recv.at[kind, step]
        return remote(slab, slab, *sems, {"row": to_row})

    def slab_arrival(kind, step):
        from_col = (col + col_count - step) % col_count
        slab = t_all.at[(sibling, across, diagonal)[kind], :, :, from_col]
        sems = slab_send.at[kind, step], slab_recv.at[kind, step]
        return remote(slab, slab, *sems, {"row": sibling})

    def hops(q, way):
        return col_count // 2 - (q + way) % 2

    def ring_block(q, half, position):
        return b_all.at[q, pl.ds(half * half_rows, half_rows), ring_column(position, col_count)]

    def ring_copy(way, q, half, hop):
        sign = 1 - 2 * way
        block = ring_block(q, half, place - sign * hop)
        to_col = ring_column(place + sign, col_count)
        sems = ring_send.at[way, q, half, hop], ring_recv.at[way, q, half, hop]
        return remote(block, block, *sems, {"col": to_col})

    def ring_arrival(way, q, half, hop):
        sign = 1 - 2 * way
        block = ring_block(q, half, place - sign * (hop + 1))
        to_col = ring_column(place + sign, col_count)
        sems = ring_send.at[way, q, half, hop], ring_recv.at[way, q, half, hop]
        return remote(block, block, *sems, {"col": to_col})

    def ring_begin(q):
        for step in range(1, row_count):
            share_arrival(q, step).wait_recv()
        near_share[q].wait()
        for half in range(2):
            for way in range(2):
                ring_copy(way, q, half, 0).start()

    def ring_step(q, half, hop):
        for way in range(2):
            if hop < hops(q, way):
                ring_arrival(way, q, half, hop).wait_recv()
                if hop + 1 < hops(q, way):
                    ring_copy(way, q, half, hop + 1).start()

    def s_copy(step):
        to_col = (col + step) % col_count
        sems = s_send.at[step - 1], s_recv.at[step - 1]
        return remote(s_ref.at[to_col], s_all.at[col], *sems, {"col": to_col})

    def s_arrival(step):
        from_col = (col + col_count - step) % col_count
        here = s_all.at[from_col]
        return remote(here, here, s_send.at[step - 1], s_recv.at[step - 1], {"col": from_col})

    def core_copy(p, m, near):
        some = pl.ds(m * block, block)
        source = part.at[sibling if near else diagonal, p, some]
        dest = core_in.at[chip if near else 1 - chip, p, some]
        sems = core_send.at[p, m, near], core_recv.at[p, m, near]
        return remote(source, dest, *sems, {"row": sibling})

    def core_arrival(p, m, near):
        here = core_in.at[chip if near else 1 - chip, p, pl.ds(m * block, block)]
        sems = core_send.at[p, m, near], core_recv.at[p, m, near]
        return remote(here, here, *sems, {"row": sibling})

    def across_copy(p, m):
        some = pl.ds(m * block, block)
        sems = across_send.at[p, m], across_recv.at[p, m]
        return remote(part.at[across, p, some], across_in.at[p, some], *sems, {"row": across})

    def across_arrival(p, m):
        here = across_in.at[p, pl.ds(m * block, block)]
        return remote(here, here, across_send.at[p, m], across_recv.at[p, m], {"row": across})

    def send_across(p, m):
        core_arrival(p, m, 0).wait_recv()

        @pl.loop(m * rows_per, (m + 1) * rows_per)
        def _(y):
            some = pl.ds(pl.multiple_of(y * a_local, a_local), a_local)
            both = part[across, p, some, :].astype(jnp.float32) + core_in[
                1 - chip, p, some, :
            ].astype(jnp.float32)
            part[across, p, some, :] = both.astype(jnp.bfloat16)

        across_copy(p, m).start()

    def swap_copy(kind, p):
        sems = swap_send.at[kind - 1, p], swap_recv.at[kind - 1, p]
        return remote(swap_out.at[kind - 1, p], swap_in.at[row, p], *sems, {"row": rows_by[kind]})

    def swap_arrival(kind, p):
        here = swap_in.at[rows_by[kind], p]
        sems = swap_send.at[kind - 1, p], swap_recv.at[kind - 1, p]
        return remote(here, here, *sems, {"row": rows_by[kind]})

    def back_copy(kind, step):
        to_col = (col + step) % col_count
        sems = back_send.at[kind, step - 1], back_recv.at[kind, step - 1]
        dest = out_ref.at[col, rows_by[kind]]
        return remote(rsym.at[kind, to_col], dest, *sems, {"col": to_col})

    def back_arrival(kind, step):
        from_col = (col + col_count - step) % col_count
        here = out_ref.at[from_col, rows_by[kind]]
        sems = back_send.at[kind, step - 1], back_recv.at[kind, step - 1]
        return remote(here, here, *sems, {"col": from_col})

    near_s = pltpu.make_async_copy(s_ref.at[col], s_all.at[col], near_sem.at[q_count + 1])
    near_share = [
        pltpu.make_async_copy(factors_ref.at[row, q], b_all.at[q, row, col], near_sem.at[q])
        for q in range(q_count)
    ]
    near_tile = pltpu.make_async_copy(
        tm_ref.at[col], t_all.at[row, :, :, col], near_sem.at[q_count]
    )
    for q in range(q_count):
        near_share[q].start()
        for step in range(1, row_count):
            share_copy(q, step).start()

    halves = mask_ref.shape[0]
    turn(table, amps_ref, tm_ref, rows, mask_ref, halves)
    near_tile.start()
    for step in range(1, col_count):
        tile_copy(step).start()

    stagger = col_count // 4

    def ring_slot(slot, half):
        q = slot // stagger
        if half == 0 and (slot + 1) % stagger == 0 and q + 1 < q_count:
            ring_begin(q + 1)
        if q < q_count:
            ring_step(q, half, slot % stagger)
        if q > 0:
            ring_step(q - 1, half, stagger + slot % stagger)

    near_tile.wait()
    slab_copy(0, 0).start()
    slab_copy(1, 0).start()
    ring_begin(0)
    turn(table, source_ref, s_ref, rows, None, halves)
    for step in range(1, col_count):
        tile_arrival(step).wait_recv()
        slab_copy(0, step).start()
        slab_copy(1, step).start()
    for slot in range(stagger):
        ring_slot(slot, 0)
        ring_slot(slot, 1)
    for step in range(col_count):
        slab_arrival(1, step).wait_recv()
        slab_copy(2, step).start()
    for slot in range(stagger, 2 * stagger):
        ring_slot(slot, 0)
        ring_slot(slot, 1)
    for step in range(col_count):
        slab_arrival(0, step).wait_recv()
        slab_arrival(2, step).wait_recv()

    for q in range(q_count):
        if q == q_count - 1:
            near_s.start()
            for step in range(1, col_count):
                s_copy(step).start()
        for p in range(slots):

            @pl.loop(0, blocks * row_count)
            def _(step):
                m, n = step // row_count, step % row_count
                left = b_all[q, pl.ds(m * rows_per, rows_per)].reshape(block, virt)
                right = t_all[n, p].reshape(virt, a_local)
                inner[
                    pl.ds(pl.multiple_of(m * block, block), block),
                    pl.ds(pl.multiple_of(n * a_local, a_local), a_local),
                ] = jnp.dot(left, right, preferred_element_type=jnp.float32).astype(jnp.bfloat16)

            if q + 1 < q_count:
                for slot in range(p * stagger // slots, (p + 1) * stagger // slots):
                    ring_slot((q + 2) * stagger + slot, 0)
            elif p > 0:
                send_across(p - 1, blocks - 1)

            for m in range(blocks):
                some = slice(m * block, (m + 1) * block)

                @pl.loop(0, blocks)
                def _(n):
                    cols = pl.ds(pl.multiple_of(n * block, block), block)
                    right = b_all[q, pl.ds(n * rows_per, rows_per)].reshape(block, virt)
                    product = lax.dot_general(
                        inner[some, :],
                        right,
                        (((1,), (1,)), ((), ())),
                        preferred_element_type=jnp.float32,
                    )
                    if q > 0:
                        product = product + total[p, some, cols]
                    if q == q_count - 1:
                        for k in range(rows_per):
                            part[n * rows_per + k, p, some, :] = product[
                                :, k * a_local : (k + 1) * a_local
                            ].astype(jnp.bfloat16)
                    else:
                        total[p, some, cols] = product

                if q == q_count - 1:
                    core_copy(p, m, 0).start()
                    core_copy(p, m, 1).start()
                    if m > 0:
                        send_across(p, m - 1)

            if q + 1 < q_count:
                for slot in range(p * stagger // slots, (p + 1) * stagger // slots):
                    ring_slot((q + 2) * stagger + slot, 1)

    send_across(slots - 1, blocks - 1)
    near_s.wait()
    for step in range(1, col_count):
        s_arrival(step).wait_recv()

    for p in range(slots):
        for y in range(row_count):
            if y % rows_per == 0:
                core_arrival(p, y // rows_per, 1).wait_recv()
                across_arrival(p, y // rows_per).wait_recv()
            for c in range(col_count):
                some = pl.ds(y * a_local + c * group, group)
                resid[p, some, :] = (
                    part[row, p, some, :].astype(jnp.float32)
                    + core_in[chip, p, some, :].astype(jnp.float32)
                    + across_in[p, some, :].astype(jnp.float32)
                    + s_all[c, p, y].astype(jnp.float32)
                )
        for kind in range(row_count - 1, -1, -1):
            some = pl.ds(pl.multiple_of(rows_by[kind] * a_local, a_local), a_local)
            turned = resid[p, some, :].T.astype(jnp.bfloat16)
            if kind == 0:
                swap_in[row, p] = turned
            else:
                swap_out[kind - 1, p] = turned
                swap_copy(kind, p).start()

    flip = 1 - (col + col_count - diagonal_from) // col_count
    for kind in range(row_count):
        y = rows_by[kind]
        if kind > 0:
            for p in range(slots):
                swap_arrival(kind, p).wait_recv()
        for p in range(slots):
            partner = p * (1 - flip) + (slots - 1 - p) * flip
            for c in range(col_count):
                some = pl.ds(pl.multiple_of(y * a_local + c * group, group), group)
                other = swap_in[y, partner, pl.ds(c * group, group), :]
                both = resid[p, some, :] + other.astype(jnp.float32)
                rsym[kind, c, p] = both.astype(jnp.bfloat16)
        for step in range(1, col_count):
            back_copy(kind, step).start()
        out_ref[col, y] = rsym[kind, col]
    for kind in range(row_count):
        for step in range(1, col_count):
            back_arrival(kind, step).wait_recv()

    for q in range(q_count):
        for step in range(1, row_count):
            share_copy(q, step).wait_send()
        for half in range(2):
            for way in range(2):
                for hop in range(hops(q, way)):
                    ring_copy(way, q, half, hop).wait_send()
    for step in range(1, col_count):
        tile_copy(step).wait_send()
        s_copy(step).wait_send()
        for kind in range(row_count):
            back_copy(kind, step).wait_send()
    for kind in range(3):
        for step in range(col_count):
            slab_copy(kind, step).wait_send()
        for p in range(slots):
            swap_copy(kind + 1, p).wait_send()
    for p in range(slots):
        for m in range(blocks):
            core_copy(p, m, 0).wait_send()
            core_copy(p, m, 1).wait_send()
            across_copy(p, m).wait_send()


def update_kernel(table, amps_ref, rsym_ref, mask_ref, occ_ref, vir_b_ref, vir_a_ref, out_ref, rows):
    pair_count, a_local = rows.shape[0], rows.shape[1]
    half_len = a_local // mask_ref.shape[0]
    for owner, pairs in enumerate(table):
        for slot, pair in enumerate(pairs):
            one = rsym_ref[owner, :, slot].reshape(LANES, a_local).astype(jnp.float32)
            rows[pair] = one.T
    known = occ_ref[...] - vir_b_ref[...]
    for half in range(mask_ref.shape[0]):

        @pl.loop(0, half_len, unroll=8)
        def _(step):
            x = half * half_len + step
            lanes = pl.ds(pl.multiple_of(x * LANES, LANES), LANES)
            denom = known - vir_a_ref[x]
            new = mask_ref[half] * (amps_ref[:, lanes].astype(jnp.float32) + rows[:, x, :] / denom)
            out_ref[:, lanes] = new.astype(jnp.bfloat16)


def params(limit=56):
    return pltpu.CompilerParams(vmem_limit_bytes=limit * 1024 * 1024)


def fast_shards(amps, source, factors, screen, occ_energy, vir_energy):
    row_count = lax.axis_size("row")
    col_count = lax.axis_size("col")
    row_id = lax.axis_index("row")
    col_id = lax.axis_index("col")
    pair_count = amps.shape[2]
    aux_count, group, virt = factors.shape
    a_local = col_count * group
    b_local = row_count * group
    occ_count = occ_energy.shape[0]
    block_count = screen.shape[1]
    block_size = virt // block_count
    halves = a_local // block_size
    per_y = block_count // row_count
    slots = pair_count // col_count
    share = aux_count // row_count
    table = pair_table(occ_count)
    bf16, f32 = jnp.bfloat16, jnp.float32

    amps = amps.reshape(pair_count, a_local * b_local)
    source = source.reshape(pair_count, a_local * b_local)
    mine = lax.dynamic_slice_in_dim(screen, row_id * halves, halves, 1)
    mine = mine.reshape(pair_count, halves, row_count, per_y)
    mine = lax.dynamic_slice_in_dim(mine, col_id * group // block_size, 1, 3)
    mask = jnp.broadcast_to(
        mine.transpose(1, 0, 2, 3).astype(f32), (halves, pair_count, row_count, group)
    ).reshape(halves, pair_count, b_local)
    occ_pair = (occ_energy[:, None] + occ_energy[None, :]).reshape(pair_count, 1)
    vir_a = lax.dynamic_slice_in_dim(vir_energy, row_id * a_local, a_local)
    vir_b = lax.dynamic_slice_in_dim(
        vir_energy.reshape(row_count, col_count, group), col_id, 1, 1
    ).reshape(1, b_local)

    block = (col_count, slots, row_count, group, a_local)
    sem = pltpu.SemaphoreType.DMA
    ring_sems = sem((2, share, 2, col_count // 2))
    back = (col_count, row_count, slots, group, a_local)
    rsym = pl.pallas_call(
        functools.partial(ladder_kernel, table, occ_count * (occ_count - 1) // 2),
        out_shape=jax.ShapeDtypeStruct(back, bf16),
        in_specs=whole(3) + [pl.BlockSpec(memory_space=pl.ANY)],
        out_specs=pl.BlockSpec(memory_space=VMEM),
        scratch_shapes=[
            VMEM((pair_count, a_local, LANES), f32),
            VMEM(block, bf16),
            VMEM(block, bf16),
            VMEM((row_count, slots, row_count, col_count, group, a_local), bf16),
            VMEM((share, row_count, col_count, group, virt), bf16),
            VMEM((virt, virt), bf16),
            VMEM((slots, virt, virt), f32),
            VMEM((row_count, slots, virt, a_local), bf16),
            VMEM((row_count // 2, slots, virt, a_local), bf16),
            VMEM((slots, virt, a_local), bf16),
            VMEM(block, bf16),
            VMEM((slots, virt, a_local), f32),
            VMEM((row_count - 1, slots, a_local, a_local), bf16),
            VMEM((row_count, slots, a_local, a_local), bf16),
            VMEM((row_count, col_count, slots, group, a_local), bf16),
            sem((share + 2,)),
            sem((share, row_count - 1)),
            sem((share, row_count - 1)),
            sem((col_count - 1,)),
            sem((col_count - 1,)),
            sem((3, col_count)),
            sem((3, col_count)),
            ring_sems,
            ring_sems,
            sem((col_count - 1,)),
            sem((col_count - 1,)),
            sem((slots, virt // 512, 2)),
            sem((slots, virt // 512, 2)),
            sem((slots, virt // 512)),
            sem((slots, virt // 512)),
            sem((row_count - 1, slots)),
            sem((row_count - 1, slots)),
            sem((row_count, col_count - 1)),
            sem((row_count, col_count - 1)),
        ],
        compiler_params=pltpu.CompilerParams(
            vmem_limit_bytes=56 * 1024 * 1024, collective_id=0, has_side_effects=True
        ),
        cost_estimate=pl.CostEstimate(
            flops=4 * share * slots * virt**3, bytes_accessed=16 * 1024 * 1024, transcendentals=0
        ),
        name="ladder",
    )(amps, source, mask, factors.reshape(row_count, share, group, virt))
    new = pl.pallas_call(
        functools.partial(update_kernel, table),
        out_shape=jax.ShapeDtypeStruct((pair_count, a_local * b_local), bf16),
        in_specs=whole(5) + [pl.BlockSpec(memory_space=pltpu.SMEM)],
        out_specs=whole(1)[0],
        scratch_shapes=[VMEM((pair_count, a_local, LANES), f32)],
        compiler_params=params(),
        name="update",
    )(amps, rsym, mask, occ_pair, vir_b, vir_a)
    return new.reshape(1, 1, pair_count, a_local * b_local)


def to_col_major(array, dim, row_count, col_count):
    old_shape = array.shape
    group_len = old_shape[dim] // (row_count * col_count)
    divided = array.reshape(
        old_shape[:dim] + (row_count, col_count, group_len) + old_shape[dim + 1 :]
    )
    return jnp.swapaxes(divided, dim, dim + 1).reshape(old_shape)


def ladder_over_aux(running, segment, left_part, right_factor):

    def step(total, factor_pair):
        left_one, right_one = factor_pair
        inner_part = jnp.einsum(
            "pcd,bd->pcb", segment, right_one, preferred_element_type=jnp.float32
        ).astype(jnp.bfloat16)
        return (
            total
            + jnp.einsum("ac,pcb->pab", left_one, inner_part, preferred_element_type=jnp.float32),
            None,
        )

    result, unused = lax.scan(step, running, (left_part, right_factor))
    return result


def shards(amps, source, factors, screen, occ_energy, vir_energy):
    row_count = lax.axis_size("row")
    col_count = lax.axis_size("col")
    row_id = lax.axis_index("row")
    col_id = lax.axis_index("col")
    pair_count = amps.shape[2]
    aux_count, group_size, virt_count = factors.shape
    a_local = col_count * group_size
    b_local = row_count * group_size
    occ_count = occ_energy.shape[0]
    block_count = screen.shape[1]
    block_size = virt_count // block_count
    a_index = row_id * a_local + jnp.arange(a_local)
    b_position = jnp.arange(b_local)
    b_index = b_position // group_size * a_local + col_id * group_size + b_position % group_size
    block_ids = jnp.arange(block_count)
    select_rows = (a_index[:, None] // block_size == block_ids[None, :]).astype(jnp.float32)
    select_cols = (b_index[:, None] // block_size == block_ids[None, :]).astype(jnp.float32)
    mask_tile = jnp.einsum("pxy,ax,by->pab", screen.astype(jnp.float32), select_rows, select_cols)
    amp_tile = amps.reshape(pair_count, a_local, b_local)
    masked = (amp_tile * mask_tile).astype(jnp.bfloat16)
    share_rows = lax.all_to_all(factors, "row", split_axis=0, concat_axis=1, tiled=True)
    col_ordered = lax.all_gather(share_rows, "col", axis=1, tiled=True)
    left_factor = to_col_major(col_ordered, 1, col_count, row_count)
    right_factor = to_col_major(col_ordered, 2, row_count, col_count)
    mine = lax.all_to_all(masked, "col", split_axis=0, concat_axis=2, tiled=True)
    initial = jnp.zeros((mine.shape[0], virt_count, virt_count), jnp.float32)
    ladder_sum = ladder_over_aux(
        initial, lax.all_gather(mine, "row", axis=1, tiled=True), left_factor, right_factor
    )
    reduced = lax.psum_scatter(
        ladder_sum.astype(jnp.bfloat16), "row", scatter_dimension=1, tiled=True
    ).astype(jnp.float32)
    ladder = lax.all_to_all(
        reduced.astype(jnp.bfloat16), "col", split_axis=2, concat_axis=0, tiled=True
    ).astype(reduced.dtype)
    resid = source.reshape(pair_count, a_local, b_local).astype(jnp.float32) + ladder
    split_tile = resid.reshape(pair_count, col_count, group_size, row_count, group_size)
    received = lax.all_to_all(
        lax.all_to_all(
            split_tile.astype(jnp.bfloat16), "row", split_axis=3, concat_axis=3, tiled=True
        ),
        "col",
        split_axis=1,
        concat_axis=1,
        tiled=True,
    ).astype(split_tile.dtype)
    swapped = received.transpose(0, 1, 4, 3, 2).reshape(occ_count, occ_count, a_local, b_local)
    swapped = swapped.transpose(1, 0, 2, 3).reshape(pair_count, a_local, b_local)
    rsym = resid + swapped
    occ_pair = (occ_energy[:, None] + occ_energy[None, :]).reshape(pair_count)
    vir_rows = lax.dynamic_slice_in_dim(vir_energy, row_id * a_local, a_local)
    vir_cols = lax.dynamic_slice_in_dim(
        vir_energy.reshape(row_count, col_count, group_size), col_id, 1, 1
    ).reshape(b_local)
    denominator = occ_pair[:, None, None] - vir_rows[None, :, None] - vir_cols[None, None, :]
    updated = mask_tile * (amp_tile.astype(jnp.float32) + rsym / denominator)
    return updated.astype(jnp.bfloat16).reshape(1, 1, pair_count, a_local * b_local)


def fits(amps, factors, screen, occ_energy, row_count, col_count):
    aux_count, rows, virt = factors.shape
    group = rows // (row_count * col_count)
    a_local, b_local = col_count * group, row_count * group
    block_size = virt // screen.shape[1]
    occ_count = occ_energy.shape[0]
    return (
        group % 16 == 0
        and b_local == LANES
        and a_local % LANES == 0
        and block_size % group == 0
        and a_local % block_size == 0
        and occ_count % 2 == 0
        and 2 * col_count == occ_count * occ_count
        and amps.shape[2] == occ_count * occ_count
        and aux_count % row_count == 0
        and aux_count >= 2 * row_count
        and row_count == 4
        and col_count % 4 == 0
        and virt % 512 == 0
        and 512 % a_local == 0
    )


def solution(mesh):
    in_specs = (
        P("row", "col", None, None),
        P("row", "col", None, None),
        P(None, ("row", "col"), None),
        P(),
        P(),
        P(),
    )
    out_specs = P("row", "col", None, None)
    row_count, col_count = mesh.shape["row"], mesh.shape["col"]

    def run(amps, source, factors, screen, occ_energy, vir_energy):
        fast = fits(amps, factors, screen, occ_energy, row_count, col_count)
        body = fast_shards if fast else shards
        return jax.shard_map(
            body, mesh=mesh, in_specs=in_specs, out_specs=out_specs, check_vma=False
        )(amps, source, factors, screen, occ_energy, vir_energy)

    return run
```

```python
import functools

import jax
import jax.numpy as jnp
from jax import lax
from jax.experimental import pallas as pl
from jax.experimental.pallas import tpu as pltpu
from jax.sharding import PartitionSpec as P

VMEM = pltpu.VMEM
LANES = 128


def pair_table(occ_count):
    table = []
    for i in range(occ_count):
        for j in range(i + 1, occ_count):
            table.append((i * occ_count + j, j * occ_count + i))
    for i in range(0, occ_count, 2):
        table.append((i * occ_count + i, (i + 1) * occ_count + i + 1))
    return table


def whole(count):
    return [pl.BlockSpec(memory_space=VMEM)] * count


def turn(table, in_ref, out_ref, rows, mask_ref, halves):
    a_local = rows.shape[1]
    groups, group = out_ref.shape[2], out_ref.shape[3]
    half_len = a_local // halves
    for half in range(halves):

        @pl.loop(0, half_len, unroll=8)
        def _(step):
            x = half * half_len + step
            one = in_ref[:, pl.ds(pl.multiple_of(x * LANES, LANES), LANES)].astype(jnp.float32)
            if mask_ref is not None:
                one = one * mask_ref[half]
            rows[:, x, :] = one

    for dest, pairs in enumerate(table):
        for slot, pair in enumerate(pairs):
            turned = rows[pair].T.astype(jnp.bfloat16)
            out_ref[dest, slot] = turned.reshape(groups, group, a_local)


def ring_column(position, count):
    position = (position + count) % count
    back = position // (count // 2)
    return (1 - back) * 2 * position + back * (2 * (count - 1 - position) + 1)


def ladder_kernel(
    table,
    diagonal_from,
    amps_ref,
    source_ref,
    screen_ref,
    factors_ref,
    out_ref,
    mask_ref,
    rows,
    tm_ref,
    s_ref,
    t_all,
    b_all,
    inner,
    total,
    part,
    core_in,
    across_in,
    s_all,
    resid,
    swap_out,
    swap_in,
    rsym,
    near_sem,
    share_send,
    share_recv,
    tile_send,
    tile_recv,
    slab_send,
    slab_recv,
    ring_send,
    ring_recv,
    s_send,
    s_recv,
    core_send,
    core_recv,
    across_send,
    across_recv,
    swap_send,
    swap_recv,
    back_send,
    back_recv,
):
    q_count, row_count, col_count, group, virt = b_all.shape
    slots, a_local = t_all.shape[1], t_all.shape[5]
    block = 512
    blocks = virt // block
    rows_per = block // a_local
    row, col = lax.axis_index("row"), lax.axis_index("col")
    sibling = row + 1 - 2 * (row % 2)
    across = (row + 2) % row_count
    diagonal = (sibling + 2) % row_count
    chip = row // 2
    rows_by = (row, sibling, across, diagonal)
    place = (col // 2) * (1 - col % 2) + (col_count - 1 - col // 2) * (col % 2)
    half_rows = row_count // 2

    def remote(source, dest, send_sem, recv_sem, device):
        return pltpu.make_async_remote_copy(
            src_ref=source,
            dst_ref=dest,
            send_sem=send_sem,
            recv_sem=recv_sem,
            device_id=device,
            device_id_type=pl.DeviceIdType.MESH,
        )

    barrier = pltpu.get_barrier_semaphore()
    for step in range(1, row_count):
        pl.semaphore_signal(
            barrier,
            inc=1,
            device_id={"row": (row + step) % row_count},
            device_id_type=pl.DeviceIdType.MESH,
        )
    for step in range(1, col_count):
        pl.semaphore_signal(
            barrier,
            inc=1,
            device_id={"col": (col + step) % col_count},
            device_id_type=pl.DeviceIdType.MESH,
        )
    pl.semaphore_wait(barrier, row_count + col_count - 2)

    def share_copy(q, step):
        to_row = (row + step) % row_count
        return remote(
            factors_ref.at[to_row, q],
            b_all.at[q, row, col],
            share_send.at[q, step - 1],
            share_recv.at[q, step - 1],
            {"row": to_row},
        )

    def share_arrival(q, step):
        from_row = (row + row_count - step) % row_count
        here = b_all.at[q, from_row, col]
        return remote(here, here, share_send.at[q, step - 1], share_recv.at[q, step - 1], {"row": from_row})

    def tile_copy(step):
        to_col = (col + step) % col_count
        return remote(
            tm_ref.at[to_col],
            t_all.at[row, :, :, col],
            tile_send.at[step - 1],
            tile_recv.at[step - 1],
            {"col": to_col},
        )

    def tile_arrival(step):
        from_col = (col + col_count - step) % col_count
        here = t_all.at[row, :, :, from_col]
        return remote(here, here, tile_send.at[step - 1], tile_recv.at[step - 1], {"col": from_col})

    def slab_copy(kind, step):
        from_col = (col + col_count - step) % col_count
        slab = t_all.at[(row, row, across)[kind], :, :, from_col]
        to_row = (sibling, across, sibling)[kind]
        sems = slab_send.at[kind, step], slab_recv.at[kind, step]
        return remote(slab, slab, *sems, {"row": to_row})

    def slab_arrival(kind, step):
        from_col = (col + col_count - step) % col_count
        slab = t_all.at[(sibling, across, diagonal)[kind], :, :, from_col]
        sems = slab_send.at[kind, step], slab_recv.at[kind, step]
        return remote(slab, slab, *sems, {"row": sibling})

    def hops(half, way):
        return col_count // 2 - (half + way) % 2

    def ring_block(q, half, position):
        return b_all.at[q, pl.ds(half * half_rows, half_rows), ring_column(position, col_count)]

    def ring_copy(way, q, half, hop):
        sign = 1 - 2 * way
        block = ring_block(q, half, place - sign * hop)
        to_col = ring_column(place + sign, col_count)
        sems = ring_send.at[way, q, half, hop], ring_recv.at[way, q, half, hop]
        return remote(block, block, *sems, {"col": to_col})

    def ring_arrival(way, q, half, hop):
        sign = 1 - 2 * way
        block = ring_block(q, half, place - sign * (hop + 1))
        to_col = ring_column(place + sign, col_count)
        sems = ring_send.at[way, q, half, hop], ring_recv.at[way, q, half, hop]
        return remote(block, block, *sems, {"col": to_col})

    def ring_begin(q):
        for step in range(1, row_count):
            share_arrival(q, step).wait_recv()
        near_share[q].wait()
        for half in range(2):
            for way in range(2):
                ring_copy(way, q, half, 0).start()

    def ring_step(q, half, hop):
        for way in range(2):
            if hop < hops(half, way):
                ring_arrival(way, q, half, hop).wait_recv()
                if hop + 1 < hops(half, way):
                    ring_copy(way, q, half, hop + 1).start()

    def s_copy(step):
        to_col = (col + step) % col_count
        sems = s_send.at[step - 1], s_recv.at[step - 1]
        return remote(s_ref.at[to_col], s_all.at[col], *sems, {"col": to_col})

    def s_arrival(step):
        from_col = (col + col_count - step) % col_count
        here = s_all.at[from_col]
        return remote(here, here, s_send.at[step - 1], s_recv.at[step - 1], {"col": from_col})

    def core_copy(p, m, near):
        some = pl.ds(m * block, block)
        source = part.at[sibling if near else diagonal, p, some]
        dest = core_in.at[chip if near else 1 - chip, p, some]
        sems = core_send.at[p, m, near], core_recv.at[p, m, near]
        return remote(source, dest, *sems, {"row": sibling})

    def core_arrival(p, m, near):
        here = core_in.at[chip if near else 1 - chip, p, pl.ds(m * block, block)]
        sems = core_send.at[p, m, near], core_recv.at[p, m, near]
        return remote(here, here, *sems, {"row": sibling})

    def across_copy(p, m):
        some = pl.ds(m * block, block)
        sems = across_send.at[p, m], across_recv.at[p, m]
        return remote(part.at[across, p, some], across_in.at[p, some], *sems, {"row": across})

    def across_arrival(p, m):
        here = across_in.at[p, pl.ds(m * block, block)]
        return remote(here, here, across_send.at[p, m], across_recv.at[p, m], {"row": across})

    def send_across(p, m):
        core_arrival(p, m, 0).wait_recv()

        @pl.loop(m * rows_per, (m + 1) * rows_per)
        def _(y):
            some = pl.ds(pl.multiple_of(y * a_local, a_local), a_local)
            both = part[across, p, some, :].astype(jnp.float32) + core_in[
                1 - chip, p, some, :
            ].astype(jnp.float32)
            part[across, p, some, :] = both.astype(jnp.bfloat16)

        across_copy(p, m).start()

    def swap_copy(kind, p):
        sems = swap_send.at[kind - 1, p], swap_recv.at[kind - 1, p]
        return remote(swap_out.at[kind - 1, p], swap_in.at[row, p], *sems, {"row": rows_by[kind]})

    def swap_arrival(kind, p):
        here = swap_in.at[rows_by[kind], p]
        sems = swap_send.at[kind - 1, p], swap_recv.at[kind - 1, p]
        return remote(here, here, *sems, {"row": rows_by[kind]})

    def back_copy(kind, step):
        to_col = (col + step) % col_count
        sems = back_send.at[kind, step - 1], back_recv.at[kind, step - 1]
        dest = out_ref.at[col, rows_by[kind]]
        return remote(rsym.at[kind, to_col], dest, *sems, {"col": to_col})

    def back_arrival(kind, step):
        from_col = (col + col_count - step) % col_count
        here = out_ref.at[from_col, rows_by[kind]]
        sems = back_send.at[kind, step - 1], back_recv.at[kind, step - 1]
        return remote(here, here, *sems, {"col": from_col})

    near_s = pltpu.make_async_copy(s_ref.at[col], s_all.at[col], near_sem.at[q_count + 1])
    near_share = [
        pltpu.make_async_copy(factors_ref.at[row, q], b_all.at[q, row, col], near_sem.at[q])
        for q in range(q_count)
    ]
    near_tile = pltpu.make_async_copy(
        tm_ref.at[col], t_all.at[row, :, :, col], near_sem.at[q_count]
    )
    for q in range(q_count):
        near_share[q].start()
        for step in range(1, row_count):
            share_copy(q, step).start()

    halves = mask_ref.shape[0]
    block_size = virt // screen_ref.shape[0]
    lane_group = lax.broadcasted_iota(jnp.int32, (1, LANES), 1) // group
    for half in range(halves):
        for pair in range(mask_ref.shape[1]):
            kept = jnp.zeros((1, LANES), jnp.float32)
            for y in range(row_count):
                one = screen_ref[row * halves + half, y * halves + col * group // block_size, pair]
                kept = jnp.where(lane_group == y, one.astype(jnp.float32), kept)
            mask_ref[half, pair : pair + 1, :] = kept
    turn(table, amps_ref, tm_ref, rows, mask_ref, halves)
    near_tile.start()
    for step in range(1, col_count):
        tile_copy(step).start()

    stagger = col_count // 4

    def ring_slot(slot, half):
        q = slot // stagger
        if half == 0 and (slot + 1) % stagger == 0 and q + 1 < q_count:
            ring_begin(q + 1)
        if q < q_count:
            ring_step(q, half, slot % stagger)
        if q > 0:
            ring_step(q - 1, half, stagger + slot % stagger)

    near_tile.wait()
    slab_copy(0, 0).start()
    slab_copy(1, 0).start()
    ring_begin(0)
    turn(table, source_ref, s_ref, rows, None, halves)
    for step in range(1, col_count):
        tile_arrival(step).wait_recv()
        slab_copy(0, step).start()
        slab_copy(1, step).start()
    for slot in range(stagger):
        ring_slot(slot, 0)
        ring_slot(slot, 1)
    for step in range(col_count):
        slab_arrival(1, step).wait_recv()
        slab_copy(2, step).start()
    for slot in range(stagger, 2 * stagger):
        ring_slot(slot, 0)
        ring_slot(slot, 1)
    for step in range(col_count):
        slab_arrival(0, step).wait_recv()
        slab_arrival(2, step).wait_recv()

    for q in range(q_count):
        if q == q_count - 1:
            near_s.start()
            for step in range(1, col_count):
                s_copy(step).start()
        for p in range(slots):

            @pl.loop(0, blocks * row_count)
            def _(step):
                m, n = step // row_count, step % row_count
                left = b_all[q, pl.ds(m * rows_per, rows_per)].reshape(block, virt)
                right = t_all[n, p].reshape(virt, a_local)
                inner[
                    pl.ds(pl.multiple_of(m * block, block), block),
                    pl.ds(pl.multiple_of(n * a_local, a_local), a_local),
                ] = jnp.dot(left, right, preferred_element_type=jnp.float32).astype(jnp.bfloat16)

            if q + 1 < q_count:
                for slot in range(p * stagger // slots, (p + 1) * stagger // slots):
                    ring_slot((q + 2) * stagger + slot, 0)
            elif p > 0:
                send_across(p - 1, blocks - 1)

            for m in range(blocks):
                some = slice(m * block, (m + 1) * block)

                @pl.loop(0, blocks)
                def _(n):
                    cols = pl.ds(pl.multiple_of(n * block, block), block)
                    right = b_all[q, pl.ds(n * rows_per, rows_per)].reshape(block, virt)
                    product = lax.dot_general(
                        inner[some, :],
                        right,
                        (((1,), (1,)), ((), ())),
                        preferred_element_type=jnp.float32,
                    )
                    if q > 0:
                        product = product + total[p, some, cols]
                    if q == q_count - 1:
                        for k in range(rows_per):
                            part[n * rows_per + k, p, some, :] = product[
                                :, k * a_local : (k + 1) * a_local
                            ].astype(jnp.bfloat16)
                    else:
                        total[p, some, cols] = product

                if q == q_count - 1:
                    core_copy(p, m, 0).start()
                    core_copy(p, m, 1).start()
                    if m > 0:
                        send_across(p, m - 1)

            if q + 1 < q_count:
                for slot in range(p * stagger // slots, (p + 1) * stagger // slots):
                    ring_slot((q + 2) * stagger + slot, 1)

    send_across(slots - 1, blocks - 1)
    near_s.wait()
    for step in range(1, col_count):
        s_arrival(step).wait_recv()

    for p in range(slots):
        for y in range(row_count):
            if y % rows_per == 0:
                core_arrival(p, y // rows_per, 1).wait_recv()
                across_arrival(p, y // rows_per).wait_recv()
            for c in range(col_count):
                some = pl.ds(y * a_local + c * group, group)
                resid[p, some, :] = (
                    part[row, p, some, :].astype(jnp.float32)
                    + core_in[chip, p, some, :].astype(jnp.float32)
                    + across_in[p, some, :].astype(jnp.float32)
                    + s_all[c, p, y].astype(jnp.float32)
                )
        for kind in range(row_count - 1, -1, -1):
            some = pl.ds(pl.multiple_of(rows_by[kind] * a_local, a_local), a_local)
            turned = resid[p, some, :].T.astype(jnp.bfloat16)
            if kind == 0:
                swap_in[row, p] = turned
            else:
                swap_out[kind - 1, p] = turned
                swap_copy(kind, p).start()

    flip = 1 - (col + col_count - diagonal_from) // col_count
    for kind in range(row_count):
        y = rows_by[kind]
        if kind > 0:
            for p in range(slots):
                swap_arrival(kind, p).wait_recv()
        for p in range(slots):
            partner = p * (1 - flip) + (slots - 1 - p) * flip
            for c in range(col_count):
                some = pl.ds(pl.multiple_of(y * a_local + c * group, group), group)
                other = swap_in[y, partner, pl.ds(c * group, group), :]
                both = resid[p, some, :] + other.astype(jnp.float32)
                rsym[kind, c, p] = both.astype(jnp.bfloat16)
        for step in range(1, col_count):
            back_copy(kind, step).start()
        out_ref[col, y] = rsym[kind, col]
    for kind in range(row_count):
        for step in range(1, col_count):
            back_arrival(kind, step).wait_recv()

    for q in range(q_count):
        for step in range(1, row_count):
            share_copy(q, step).wait_send()
        for half in range(2):
            for way in range(2):
                for hop in range(hops(half, way)):
                    ring_copy(way, q, half, hop).wait_send()
    for step in range(1, col_count):
        tile_copy(step).wait_send()
        s_copy(step).wait_send()
        for kind in range(row_count):
            back_copy(kind, step).wait_send()
    for kind in range(3):
        for step in range(col_count):
            slab_copy(kind, step).wait_send()
        for p in range(slots):
            swap_copy(kind + 1, p).wait_send()
    for p in range(slots):
        for m in range(blocks):
            core_copy(p, m, 0).wait_send()
            core_copy(p, m, 1).wait_send()
            across_copy(p, m).wait_send()


def update_kernel(table, amps_ref, rsym_ref, mask_ref, occ_ref, vir_ref, out_ref, rows):
    pair_count, a_local = rows.shape[0], rows.shape[1]
    half_len = a_local // mask_ref.shape[0]
    for owner, pairs in enumerate(table):
        for slot, pair in enumerate(pairs):
            one = rsym_ref[owner, :, slot].reshape(LANES, a_local).astype(jnp.float32)
            rows[pair] = one.T
    col_count, row_count, group = rsym_ref.shape[0], rsym_ref.shape[1], rsym_ref.shape[3]
    occ_count = occ_ref.shape[0]
    row, col = lax.axis_index("row"), lax.axis_index("col")
    lane = lax.broadcasted_iota(jnp.int32, (8, LANES), 1)
    pair_of = lax.broadcasted_iota(jnp.int32, (pair_count, LANES), 0)

    def with_lane(y, vir_b):
        b = y // group * a_local + col * group + y % group
        return jnp.where(lane == y, vir_ref[b], vir_b)

    vir_b = lax.fori_loop(0, LANES, with_lane, jnp.zeros((8, LANES), jnp.float32), unroll=8)
    known = jnp.zeros((pair_count, LANES), jnp.float32)
    for pair in range(pair_count):
        occ_pair = occ_ref[pair // occ_count] + occ_ref[pair % occ_count]
        known = jnp.where(pair_of == pair, occ_pair, known)
    known = known - vir_b[:1]
    for half in range(mask_ref.shape[0]):

        @pl.loop(0, half_len, unroll=8)
        def _(step):
            x = half * half_len + step
            lanes = pl.ds(pl.multiple_of(x * LANES, LANES), LANES)
            denom = known - vir_ref[row * a_local + x]
            new = mask_ref[half] * (amps_ref[:, lanes].astype(jnp.float32) + rows[:, x, :] / denom)
            out_ref[:, lanes] = new.astype(jnp.bfloat16)


def params(limit=56):
    return pltpu.CompilerParams(vmem_limit_bytes=limit * 1024 * 1024)


def fast_shards(amps, source, factors, screen, occ_energy, vir_energy):
    row_count = lax.axis_size("row")
    col_count = lax.axis_size("col")
    pair_count = amps.shape[2]
    aux_count, group, virt = factors.shape
    a_local = col_count * group
    b_local = row_count * group
    occ_count = occ_energy.shape[0]
    block_count = screen.shape[1]
    block_size = virt // block_count
    halves = a_local // block_size
    slots = pair_count // col_count
    share = aux_count // row_count
    table = pair_table(occ_count)
    bf16, f32 = jnp.bfloat16, jnp.float32

    amps = amps.reshape(pair_count, a_local * b_local)
    source = source.reshape(pair_count, a_local * b_local)
    block = (col_count, slots, row_count, group, a_local)
    sem = pltpu.SemaphoreType.DMA
    ring_sems = sem((2, share, 2, col_count // 2))
    back = (col_count, row_count, slots, group, a_local)
    rsym, mask = pl.pallas_call(
        functools.partial(ladder_kernel, table, occ_count * (occ_count - 1) // 2),
        out_shape=[
            jax.ShapeDtypeStruct(back, bf16),
            jax.ShapeDtypeStruct((halves, pair_count, b_local), f32),
        ],
        in_specs=whole(2)
        + [pl.BlockSpec(memory_space=pltpu.SMEM), pl.BlockSpec(memory_space=pl.ANY)],
        out_specs=whole(2),
        scratch_shapes=[
            VMEM((pair_count, a_local, LANES), f32),
            VMEM(block, bf16),
            VMEM(block, bf16),
            VMEM((row_count, slots, row_count, col_count, group, a_local), bf16),
            VMEM((share, row_count, col_count, group, virt), bf16),
            VMEM((virt, virt), bf16),
            VMEM((slots, virt, virt), f32),
            VMEM((row_count, slots, virt, a_local), bf16),
            VMEM((row_count // 2, slots, virt, a_local), bf16),
            VMEM((slots, virt, a_local), bf16),
            VMEM(block, bf16),
            VMEM((slots, virt, a_local), f32),
            VMEM((row_count - 1, slots, a_local, a_local), bf16),
            VMEM((row_count, slots, a_local, a_local), bf16),
            VMEM((row_count, col_count, slots, group, a_local), bf16),
            sem((share + 2,)),
            sem((share, row_count - 1)),
            sem((share, row_count - 1)),
            sem((col_count - 1,)),
            sem((col_count - 1,)),
            sem((3, col_count)),
            sem((3, col_count)),
            ring_sems,
            ring_sems,
            sem((col_count - 1,)),
            sem((col_count - 1,)),
            sem((slots, virt // 512, 2)),
            sem((slots, virt // 512, 2)),
            sem((slots, virt // 512)),
            sem((slots, virt // 512)),
            sem((row_count - 1, slots)),
            sem((row_count - 1, slots)),
            sem((row_count, col_count - 1)),
            sem((row_count, col_count - 1)),
        ],
        compiler_params=pltpu.CompilerParams(
            vmem_limit_bytes=56 * 1024 * 1024, collective_id=0, has_side_effects=True
        ),
        cost_estimate=pl.CostEstimate(
            flops=4 * share * slots * virt**3, bytes_accessed=16 * 1024 * 1024, transcendentals=0
        ),
        name="ladder",
    )(amps, source, screen.transpose(1, 2, 0), factors.reshape(row_count, share, group, virt))
    new = pl.pallas_call(
        functools.partial(update_kernel, table),
        out_shape=jax.ShapeDtypeStruct((pair_count, a_local * b_local), bf16),
        in_specs=whole(3) + [pl.BlockSpec(memory_space=pltpu.SMEM)] * 2,
        out_specs=whole(1)[0],
        scratch_shapes=[VMEM((pair_count, a_local, LANES), f32)],
        compiler_params=params(),
        name="update",
    )(amps, rsym, mask, occ_energy, vir_energy)
    return new.reshape(1, 1, pair_count, a_local * b_local)


def to_col_major(array, dim, row_count, col_count):
    old_shape = array.shape
    group_len = old_shape[dim] // (row_count * col_count)
    divided = array.reshape(
        old_shape[:dim] + (row_count, col_count, group_len) + old_shape[dim + 1 :]
    )
    return jnp.swapaxes(divided, dim, dim + 1).reshape(old_shape)


def ladder_over_aux(running, segment, left_part, right_factor):

    def step(total, factor_pair):
        left_one, right_one = factor_pair
        inner_part = jnp.einsum(
            "pcd,bd->pcb", segment, right_one, preferred_element_type=jnp.float32
        ).astype(jnp.bfloat16)
        return (
            total
            + jnp.einsum("ac,pcb->pab", left_one, inner_part, preferred_element_type=jnp.float32),
            None,
        )

    result, unused = lax.scan(step, running, (left_part, right_factor))
    return result


def shards(amps, source, factors, screen, occ_energy, vir_energy):
    row_count = lax.axis_size("row")
    col_count = lax.axis_size("col")
    row_id = lax.axis_index("row")
    col_id = lax.axis_index("col")
    pair_count = amps.shape[2]
    aux_count, group_size, virt_count = factors.shape
    a_local = col_count * group_size
    b_local = row_count * group_size
    occ_count = occ_energy.shape[0]
    block_count = screen.shape[1]
    block_size = virt_count // block_count
    a_index = row_id * a_local + jnp.arange(a_local)
    b_position = jnp.arange(b_local)
    b_index = b_position // group_size * a_local + col_id * group_size + b_position % group_size
    block_ids = jnp.arange(block_count)
    select_rows = (a_index[:, None] // block_size == block_ids[None, :]).astype(jnp.float32)
    select_cols = (b_index[:, None] // block_size == block_ids[None, :]).astype(jnp.float32)
    mask_tile = jnp.einsum("pxy,ax,by->pab", screen.astype(jnp.float32), select_rows, select_cols)
    amp_tile = amps.reshape(pair_count, a_local, b_local)
    masked = (amp_tile * mask_tile).astype(jnp.bfloat16)
    share_rows = lax.all_to_all(factors, "row", split_axis=0, concat_axis=1, tiled=True)
    col_ordered = lax.all_gather(share_rows, "col", axis=1, tiled=True)
    left_factor = to_col_major(col_ordered, 1, col_count, row_count)
    right_factor = to_col_major(col_ordered, 2, row_count, col_count)
    mine = lax.all_to_all(masked, "col", split_axis=0, concat_axis=2, tiled=True)
    initial = jnp.zeros((mine.shape[0], virt_count, virt_count), jnp.float32)
    ladder_sum = ladder_over_aux(
        initial, lax.all_gather(mine, "row", axis=1, tiled=True), left_factor, right_factor
    )
    reduced = lax.psum_scatter(
        ladder_sum.astype(jnp.bfloat16), "row", scatter_dimension=1, tiled=True
    ).astype(jnp.float32)
    ladder = lax.all_to_all(
        reduced.astype(jnp.bfloat16), "col", split_axis=2, concat_axis=0, tiled=True
    ).astype(reduced.dtype)
    resid = source.reshape(pair_count, a_local, b_local).astype(jnp.float32) + ladder
    split_tile = resid.reshape(pair_count, col_count, group_size, row_count, group_size)
    received = lax.all_to_all(
        lax.all_to_all(
            split_tile.astype(jnp.bfloat16), "row", split_axis=3, concat_axis=3, tiled=True
        ),
        "col",
        split_axis=1,
        concat_axis=1,
        tiled=True,
    ).astype(split_tile.dtype)
    swapped = received.transpose(0, 1, 4, 3, 2).reshape(occ_count, occ_count, a_local, b_local)
    swapped = swapped.transpose(1, 0, 2, 3).reshape(pair_count, a_local, b_local)
    rsym = resid + swapped
    occ_pair = (occ_energy[:, None] + occ_energy[None, :]).reshape(pair_count)
    vir_rows = lax.dynamic_slice_in_dim(vir_energy, row_id * a_local, a_local)
    vir_cols = lax.dynamic_slice_in_dim(
        vir_energy.reshape(row_count, col_count, group_size), col_id, 1, 1
    ).reshape(b_local)
    denominator = occ_pair[:, None, None] - vir_rows[None, :, None] - vir_cols[None, None, :]
    updated = mask_tile * (amp_tile.astype(jnp.float32) + rsym / denominator)
    return updated.astype(jnp.bfloat16).reshape(1, 1, pair_count, a_local * b_local)


def fits(amps, factors, screen, occ_energy, row_count, col_count):
    aux_count, rows, virt = factors.shape
    group = rows // (row_count * col_count)
    a_local, b_local = col_count * group, row_count * group
    block_size = virt // screen.shape[1]
    occ_count = occ_energy.shape[0]
    return (
        group % 16 == 0
        and b_local == LANES
        and a_local % LANES == 0
        and block_size % group == 0
        and a_local % block_size == 0
        and occ_count % 2 == 0
        and 2 * col_count == occ_count * occ_count
        and amps.shape[2] == occ_count * occ_count
        and aux_count % row_count == 0
        and aux_count >= 2 * row_count
        and row_count == 4
        and col_count % 4 == 0
        and virt % 512 == 0
        and 512 % a_local == 0
    )


def solution(mesh):
    in_specs = (
        P("row", "col", None, None),
        P("row", "col", None, None),
        P(None, ("row", "col"), None),
        P(),
        P(),
        P(),
    )
    out_specs = P("row", "col", None, None)
    row_count, col_count = mesh.shape["row"], mesh.shape["col"]

    def run(amps, source, factors, screen, occ_energy, vir_energy):
        fast = fits(amps, factors, screen, occ_energy, row_count, col_count)
        body = fast_shards if fast else shards
        return jax.shard_map(
            body, mesh=mesh, in_specs=in_specs, out_specs=out_specs, check_vma=False
        )(amps, source, factors, screen, occ_energy, vir_energy)

    return run
```
